512 devices in a mesh: dp: 32 (over y, z_lo, core), pipe: 16 (over z_hi, x).
Axes of the slice: x: 4, y: 8, z: 8 (z_hi: 4, z_lo: 2; z = z_hi * 2 + z_lo), core: 2. Of those that a mesh axis runs over, the one named last changes fastest.
Arguments:
- hidden: bfloat16 [2, 128, 8192], P(None, 'pipe', 'dp'), may hold values from -180 to 180
- weight: bfloat16 [65536, 8192], P('pipe', 'dp'), may hold values from -0.25 to 0.25
- targets: int32 [2, 128], replicated, may hold values from 0 to 65535
- row_grad: float32 [2, 128], replicated, may hold values from 4 to 40
Outputs:
- grad_hidden: bfloat16 [2, 128, 8192], P(None, 'pipe', 'dp')
- grad_weight: bfloat16 [65536, 8192], P('pipe', 'dp')
- row_loss: float32 [2, 128], P(None, 'dp')
The draws below stay inside these ranges and needn't reach their ends.
All inputs are finite; a program needn't handle non-finite values.
Results may differ from the reference program's by a relative error of at most 0.006.
Values may be sent and summed in bfloat16 or wider, within the bound.
A program may use at most 64 MiB of HBM per device.

```python
import math
import jax
import jax.numpy as jnp
import numpy as np
from jax import lax

D = 8192
MB = 128
VOCAB = 65536


def draw_hidden(key, part):
    key = jax.random.fold_in(key, 11)
    base_key = jax.random.fold_in(key, 0)
    base = jnp.clip(jax.random.normal(base_key, (2, MB, D), jnp.float32), -6.0, 6.0)
    return base.astype(jnp.bfloat16)


def with_ends(drawn, own_key, least, largest):
    extent = drawn.shape
    place = [jax.random.randint(jax.random.fold_in(own_key, axis), (), 0, extent[axis]) for axis in range(len(extent))]
    drawn = drawn.at[tuple(place)].set(least)
    longest = extent.index(max(extent))
    place[longest] = (place[longest] + 1) % extent[longest]
    return drawn.at[tuple(place)].set(largest)


def levels(stream_key, extent, shards, least, top_value):
    factor_of = 1.0
    for axis_at, shards_of in shards:
        heights = jax.random.uniform(jax.random.fold_in(jax.random.fold_in(stream_key, 6), axis_at), (shards_of,), jnp.float32, least / len(shards), top_value / len(shards))
        factor_of = factor_of * jnp.repeat(jnp.exp(heights), extent[axis_at] // shards_of).reshape((-1,) + (1,) * (len(extent) - 1 - axis_at))
    return factor_of


def cumulative_ranks(number_of, slope):
    weights = [(1 << 20) // math.isqrt(rank ** slope) + 1 for rank in range(1, number_of + 1)]
    scale = 1 + sum(weights) // (1 << 30)
    return np.cumsum(np.array([max(1, weight // scale) for weight in weights]))


def skewed_ids(key, dims, count, lean):
    table = cumulative_ranks(count, lean)
    ticket = jax.random.randint(jax.random.fold_in(key, 1), dims, 0, int(table[count - 1]))
    grade = jnp.searchsorted(jnp.asarray(table, jnp.int32), ticket, side="right")
    return jax.random.permutation(jax.random.fold_in(key, 2), count)[grade].astype(jnp.int32)


def noise(rng, extent, width, reach, cuts=(), held_as=jnp.bfloat16):
    drawn = width * jax.random.normal(rng, extent, jnp.float32)
    if cuts:
        drawn = drawn * levels(rng, extent, cuts, -0.22, 0.18)
    return jnp.clip(drawn, -reach, reach).astype(held_as)


def setup_inputs(seed: int = 0) -> dict:
    splits = jax.random.split(jax.random.key(seed), 5)
    hidden = draw_hidden(jax.random.fold_in(splits[4], 71), 0)
    weight = noise(splits[1], (VOCAB, D), (D // 16) ** -0.5, 0.25, ((0, 16), (1, 32)))
    targets = with_ends(skewed_ids(splits[2], (2, MB), VOCAB, 2), jax.random.fold_in(splits[2], 3), 0, VOCAB - 1).astype(jnp.int32)
    row_grad = jnp.clip(jnp.exp(jax.random.uniform(splits[3], (2, MB), jnp.float32, math.log(4.0), math.log(40.0))), 4.0, 40.0)
    return {"hidden": hidden, "weight": weight, "targets": targets, "row_grad": row_grad}


def reference(hidden, weight, targets, row_grad):
    grad_weight = jnp.zeros(weight.shape, jnp.float32)
    grads = []
    losses = []
    for micro in range(2):
        rows = hidden[micro]
        logits = lax.dot_general(rows, weight, (((1,), (1,)), ((), ())), preferred_element_type=jnp.float32)
        top = jnp.max(logits, axis=1)
        total = jnp.sum(jnp.exp(logits - top[:, None]), axis=1)
        picked = jnp.take_along_axis(logits, targets[micro][:, None].astype(jnp.int32), axis=1)[:, 0]
        losses.append(top + jnp.log(total) - picked)
        vocab_ids = jnp.arange(weight.shape[0], dtype=jnp.int32)
        hit = (targets[micro][:, None] == vocab_ids[None, :]).astype(jnp.float32)
        probs = jnp.exp(logits - top[:, None]) / total[:, None]
        dlogits = (row_grad[micro][:, None] * (probs - hit)).astype(jnp.bfloat16)
        grads.append(jnp.dot(dlogits, weight, preferred_element_type=jnp.float32).astype(jnp.bfloat16))
        grad_weight = grad_weight + lax.dot_general(dlogits, rows, (((0,), (0,)), ((), ())), preferred_element_type=jnp.float32)
    return jnp.stack(grads), grad_weight.astype(jnp.bfloat16), jnp.stack(losses)
```

```python
import functools
import math

import jax
import jax.numpy as jnp
from jax import lax
from jax.experimental import pallas as pl
from jax.experimental.pallas import tpu as pltpu
from jax.sharding import PartitionSpec as P

MESH = pl.DeviceIdType.MESH
F32, BF16, I16, I32 = jnp.float32, jnp.bfloat16, jnp.int16, jnp.int32

Y, NB, ROWS = 8, 16, 16
HALF = 2048
SUB, NSUB = 1024, 2
CODE = 128
STEP = math.log(2.0) / 256
TOP = 32766.0
CHUNK = 256


def coords():
    dp, pipe = lax.axis_index("dp"), lax.axis_index("pipe")
    return dp // 4, (dp // 2) % 2, dp % 2, pipe


def lanes_mul(x, s):
    n = x.shape[1] // 128
    return jnp.concatenate([x[:, i * 128 : (i + 1) * 128] * s for i in range(n)], axis=1)


def encode(ref, slot, x, bound):
    code = jnp.ceil(jnp.log(jnp.maximum(bound, 1e-30)) * (1.0 / STEP)) + 1.0
    inv = TOP * jnp.exp(code * -STEP)
    ref[slot, :, :SUB] = jnp.round(lanes_mul(x, inv)).astype(I32).astype(I16)
    ref[slot, :, SUB:] = code.astype(I32).astype(I16)


def decode(ref, slot):
    scale = jnp.exp(ref[slot, :, SUB:].astype(I32).astype(F32) * STEP)
    x = ref[slot, :, :SUB].astype(I32).astype(F32)
    return lanes_mul(x, scale * (1.0 / TOP)), scale


def diagonal():
    return lax.broadcasted_iota(I32, (ROWS, 128), 0) == lax.broadcasted_iota(I32, (ROWS, 128), 1)


def to_lanes(col):
    return jnp.sum(jnp.where(diagonal(), col, 0.0), axis=0, keepdims=True)


def to_rows(row):
    shape = row.shape[:-2] + (ROWS, 128)
    at = len(shape) - 2
    eye = lax.broadcasted_iota(I32, shape, at) == lax.broadcasted_iota(I32, shape, at + 1)
    return jnp.broadcast_to(
        jnp.sum(jnp.where(eye, jnp.broadcast_to(row, shape), 0.0), axis=-1, keepdims=True), shape
    )


def kernel(
    h_ref, w_ref, t_ref, g_ref, dh_ref, dw_ref, loss_ref,
    hm, hs, wm, ws, part, scale, tcol, gcol, logit, e_all, dl, dwv, acc, fcol,
    zs, zr, ls, lr, ss, sr, st0, st1, st2, mine, dhs, dhr,
    w_sem, ws_sem, hl_sem, h_send, h_recv, hf_send, hf_recv, z_send, z_recv, l_send, l_recv, s_send, s_recv,
    st_send, st_recv, az_send, az_recv, al_send, al_recv, as_send, as_recv, ac_send, ac_recv,
    d_send, d_recv, dw_sem,
):
    y, zl, c, pipe = coords()
    zh, px = pipe // 4, pipe % 4
    me_dp = y * 4 + zl * 2 + c

    def at_dp(yy, zz, cc):
        return (yy * 4 + zz * 2 + cc, pipe)

    def yo(o):
        return lax.rem(y + o + Y, Y)

    def pipe_peer(i):
        return lax.rem(zh + i // 4, 4) * 4 + lax.rem(px + i % 4, 4)

    def dp_peer(i):
        return lax.rem(y + i // 2, Y), lax.rem(zl + i % 2, 2)

    sib = at_dp(y, zl, 1 - c)
    zdev = at_dp(y, 1 - zl, c)

    def send(src, dst, s_sem, r_sem, dev):
        cp = pltpu.make_async_remote_copy(
            src_ref=src, dst_ref=dst, send_sem=s_sem, recv_sem=r_sem, device_id=dev, device_id_type=MESH
        )
        cp.start()
        return cp

    w_copy = pltpu.make_async_copy(w_ref, wm, w_sem)
    w_copy.start()
    h_copy = pltpu.make_async_copy(h_ref, hm.at[pipe], hl_sem)
    h_copy.start()

    barrier = pltpu.get_barrier_semaphore()

    @pl.loop(1, 16)
    def _(i):
        pl.semaphore_signal(barrier, inc=1, device_id=(me_dp, pipe_peer(i)), device_id_type=MESH)
        yy, zz = dp_peer(i)
        pl.semaphore_signal(barrier, inc=1, device_id=at_dp(yy, zz, c), device_id_type=MESH)

    pl.semaphore_signal(barrier, inc=1, device_id=sib, device_id_type=MESH)

    shape = (NB, ROWS, 128)
    b_id, r_id = lax.broadcasted_iota(I32, shape, 0), lax.broadcasted_iota(I32, shape, 1)
    lane = lax.broadcasted_iota(I32, shape, 2)
    pick = lane == b_id * 8 + r_id % 8
    first = r_id < 8

    def column(ref):
        x = ref[...].astype(F32)
        x = jnp.where(first, x[0:1].reshape(1, 1, 128), x[1:2].reshape(1, 1, 128))
        return jnp.broadcast_to(jnp.sum(jnp.where(pick, x, 0.0), axis=-1, keepdims=True), shape)

    tcol[...] = column(t_ref).astype(I32)
    gcol[...] = column(g_ref)

    pl.semaphore_wait(barrier, 31)

    h_copy.wait()

    @pl.loop(1, 16)
    def _(i):
        send(hm.at[pipe], hm.at[pipe], h_send, h_recv.at[i // 4], (me_dp, pipe_peer(i)))

    half_rows = pl.ds(pl.multiple_of((1 - c) * HALF, HALF), HALF)
    w_swap = send(w_ref.at[half_rows], ws, ws_sem.at[0], ws_sem.at[1], sib)

    forwards = []
    for n, dz in enumerate((0, 1, 3, 2)):
        group = pl.ds(lax.rem(zh + 4 - dz, 4) * 4, 4)
        count = 3 if dz == 0 else 4
        some = hm.at[pl.ds(0, count)]
        pltpu.make_async_copy(some, some, h_recv.at[dz]).wait()
        forwards.append(send(hm.at[group], hs.at[group], hf_send.at[n], hf_recv.at[n], sib))
    for n, dz in enumerate((0, 1, 3, 2)):
        group = pl.ds(lax.rem(zh + 4 - dz, 4) * 4, 4)
        forwards[n].wait_recv()
    w_copy.wait()
    w_swap.wait_recv()

    scale[...] = jnp.zeros(shape, F32)
    hm_all = hm[...].reshape(NB * ROWS, CHUNK)
    hs_all = hs[...].reshape(NB * ROWS, CHUNK)
    nt = (((1,), (1,)), ((), ()))

    @pl.loop(0, HALF // CHUNK)
    def _(k):
        own = pl.ds(pl.multiple_of(c * HALF + k * CHUNK, CHUNK), CHUNK)
        there = pl.ds(pl.multiple_of(k * CHUNK, CHUNK), CHUNK)
        x = lax.dot_general(hm[...].reshape(NB * ROWS, CHUNK), wm[own, :], nt, preferred_element_type=F32)
        x += lax.dot_general(hs[...].reshape(NB * ROWS, CHUNK), ws[there, :], nt, preferred_element_type=F32)
        x = x.reshape(NB, ROWS, CHUNK)
        part[:, :, there] = x
        scale[...] = jnp.maximum(scale[...], jnp.maximum(jnp.abs(x[..., :128]), jnp.abs(x[..., 128:])))

    scale[...] = jnp.broadcast_to(jnp.max(scale[...], axis=-1, keepdims=True), shape)

    signs = (1, -1)
    order = (4, 3, -3, 2, -2, 1, -1, 0)
    pending = []

    def block(o, zz):
        return yo(o) * 2 + zz

    def own_part(b, u):
        return part[b, :, u * SUB : (u + 1) * SUB]

    zsend, zrecv = {}, {}
    for n, o in enumerate(order):
        for u in range(NSUB):
            b = block(o * signs[u], 1 - zl)
            slot = n * NSUB + u
            encode(zs, slot, own_part(b, u), scale[b])
            zrecv[o, u] = send(zs.at[slot], zr.at[slot], z_send.at[slot], z_recv.at[slot], zdev)
            pending.append(zrecv[o, u])

    def with_z(o, u):
        b = block(o * signs[u], zl)
        slot = order.index(o) * NSUB + u
        zrecv[o, u].wait_recv()
        x, s = decode(zr, slot)
        return own_part(b, u) + x, scale[b] + s

    long, short = {}, {}
    for k in range(1, 5):
        for u in range(NSUB):
            x, s = with_z(5 - k, u)
            slot = (k - 1) * NSUB + u
            if k > 1:
                long[k - 1, u].wait_recv()
                more, more_s = decode(lr, slot - NSUB)
                x, s = x + more, s + more_s
            encode(ls, slot, x, s)
            long[k, u] = send(
                ls.at[slot], lr.at[slot], l_send.at[slot], l_recv.at[slot], at_dp(yo(signs[u]), zl, c)
            )
            pending.append(long[k, u])
        if k > 3:
            continue
        for u in range(NSUB):
            x, s = with_z(k - 4, u)
            slot = (k - 1) * NSUB + u
            if k > 1:
                short[k - 1, u].wait_recv()
                more, more_s = decode(sr, slot - NSUB)
                x, s = x + more, s + more_s
            encode(ss, slot, x, s)
            short[k, u] = send(
                ss.at[slot], sr.at[slot], s_send.at[slot], s_recv.at[slot], at_dp(yo(-signs[u]), zl, c)
            )
            pending.append(short[k, u])
    for u in range(NSUB):
        x, _ = with_z(0, u)
        short[3, u].wait_recv()
        x += decode(sr, 2 * NSUB + u)[0]
        long[4, u].wait_recv()
        x += decode(lr, 3 * NSUB + u)[0]
        logit[:, u * SUB : (u + 1) * SUB] = x

    mb = y * 2 + zl
    x = logit[...]
    m_col = jnp.max(x, axis=1, keepdims=True)
    e = jnp.exp(x - m_col)
    s_col = jnp.sum(e, axis=1, keepdims=True)
    ids = pipe * (2 * HALF) + c * HALF + lax.broadcasted_iota(I32, x.shape, 1)
    hit = ids == jnp.concatenate([tcol[mb]] * (HALF // 128), axis=1)
    p_col = jnp.sum(jnp.where(hit, x, 0.0), axis=1, keepdims=True)
    for u in range(NSUB):
        e_all[c, u, mb] = e[:, u * SUB : (u + 1) * SUB].astype(BF16)

    wide = (ROWS, 128)
    stats = [to_lanes(jnp.broadcast_to(v, wide)) for v in (m_col, s_col, p_col)]

    glong, gshort, gz = {}, {}, {}

    def chunk(u, b):
        return e_all.at[c, u, b]

    def to_core(u, b, n):
        cp = send(chunk(u, b), chunk(u, b), ac_send, ac_recv, sib)
        return cp

    def to_z(u, o):
        b = block(o * signs[u], zl)
        slot = order.index(o) * NSUB + u
        gz[o, u] = send(chunk(u, b), chunk(u, b), az_send.at[slot], az_recv.at[slot], zdev)
        pending.append(gz[o, u])

    def from_z(u, o):
        b = block(o * signs[u], 1 - zl)
        slot = order.index(o) * NSUB + u
        pltpu.make_async_copy(chunk(u, b), chunk(u, b), az_recv.at[slot]).wait()
        to_core(u, b, slot)

    def go_long(u, k):
        b = block(-(k - 1) * signs[u], zl)
        slot = (k - 1) * NSUB + u
        glong[k, u] = send(chunk(u, b), chunk(u, b), al_send.at[slot], al_recv.at[slot], at_dp(yo(signs[u]), zl, c))
        pending.append(glong[k, u])

    def go_short(u, k):
        b = block((k - 1) * signs[u], zl)
        slot = (k - 1) * NSUB + u
        gshort[k, u] = send(chunk(u, b), chunk(u, b), as_send.at[slot], as_recv.at[slot], at_dp(yo(-signs[u]), zl, c))
        pending.append(gshort[k, u])

    def got(sem, slot, u, b):
        pltpu.make_async_copy(chunk(u, b), chunk(u, b), sem.at[slot]).wait()

    def step(k):
        for u in range(NSUB):
            b = block(-k * signs[u], zl)
            got(al_recv, (k - 1) * NSUB + u, u, b)
            if k < 4:
                go_long(u, k + 1)
            to_z(u, -k if k < 4 else 4)
            to_core(u, b, None)
        if k < 4:
            for u in range(NSUB):
                b = block(k * signs[u], zl)
                got(as_recv, (k - 1) * NSUB + u, u, b)
                if k < 3:
                    go_short(u, k + 1)
                to_z(u, k)
                to_core(u, b, None)

    for u in range(NSUB):
        go_long(u, 1)
        go_short(u, 1)
        to_z(u, 0)
        to_core(u, mb, None)

    for n in range(3):
        mine[0, :, n * 128 : (n + 1) * 128] = stats[n]
    both = send(mine.at[0], st0.at[0], st_send.at[0], st_recv.at[0], sib)
    pending.append(both)
    both.wait_recv()
    other = [st0[0, :, n * 128 : (n + 1) * 128] for n in range(3)]
    m_two = jnp.maximum(stats[0], other[0])
    s_two = stats[1] * jnp.exp(stats[0] - m_two) + other[1] * jnp.exp(other[0] - m_two)
    p_two = stats[2] + other[2]
    for n, v in enumerate((m_two, s_two, p_two)):
        st1[pipe, :, n * 128 : (n + 1) * 128] = v

    @pl.loop(1, 16)
    def _(i):
        send(st1.at[pipe], st1.at[pipe], st_send.at[1], st_recv.at[1], (me_dp, pipe_peer(i)))

    step(1)
    for u in range(NSUB):
        from_z(u, 0)
    step(2)

    fifteen = st1.at[pl.ds(0, 15)]
    pltpu.make_async_copy(fifteen, fifteen, st_recv.at[1]).wait()
    ms, sums, picks = (st1[:, 0, n * 128 : (n + 1) * 128] for n in range(3))
    top = jnp.max(ms, axis=0, keepdims=True)
    total = jnp.sum(sums * jnp.exp(ms - top), axis=0, keepdims=True)
    picked = jnp.sum(picks, axis=0, keepdims=True)
    live = lax.broadcasted_iota(I32, (1, 128), 1) < ROWS
    total = jnp.where(live, total, 1.0)
    g = to_lanes(gcol[mb])
    f_mine = g * (jnp.exp(stats[0] - top) / total)
    f_other = g * (jnp.exp(other[0] - top) / total)
    at_hit = g * (jnp.exp(picked - top) / total - 1.0)
    loss = top + jnp.log(total) - picked
    is0 = c == 0
    st2[mb, :, 0:128] = jnp.where(is0, f_mine, f_other)
    st2[mb, :, 128:256] = jnp.where(is0, f_other, f_mine)
    st2[mb, :, 256:384] = at_hit

    @pl.loop(1, 16)
    def _(i):
        yy, zz = dp_peer(i)
        send(st2.at[mb], st2.at[mb], st_send.at[2], st_recv.at[2], at_dp(yy, zz, c))

    loss_col = to_rows(loss)
    r2, l2 = lax.broadcasted_iota(I32, wide, 0), lax.broadcasted_iota(I32, wide, 1)
    loss_out = jnp.where(r2 % 8 == 4 * c + l2, loss_col, 0.0).reshape(2, 8, 128)
    loss_ref[...] = jnp.sum(loss_out, axis=1)[:, 0:4]

    for u in range(NSUB):
        from_z(u, -1)
        from_z(u, 1)
    step(3)
    for u in range(NSUB):
        from_z(u, -2)
        from_z(u, 2)
    step(4)
    for u in range(NSUB):
        from_z(u, -3)
        from_z(u, 3)

    fifteen2 = st2.at[pl.ds(0, 15)]
    pltpu.make_async_copy(fifteen2, fifteen2, st_recv.at[2]).wait()
    for n in range(3):
        fcol[n] = to_rows(st2[:, :, n * 128 : (n + 1) * 128])
    for u in range(NSUB):
        from_z(u, 4)
    there = e_all.at[1 - c]
    pltpu.make_async_copy(there, there, ac_recv).wait()

    acc[...] = jnp.zeros(acc.shape, F32)
    full = (NB * ROWS, CHUNK)

    def twice(x):
        x = x.reshape(NB * ROWS, 128)
        return jnp.concatenate([x, x], axis=1)

    @pl.loop(0, 2 * HALF // CHUNK)
    def _(q):
        hh, u, k = q // 8, (q // 4) % 2, q % 4
        lanes = pl.ds(pl.multiple_of(k * CHUNK, CHUNK), CHUNK)
        e = e_all[hh, u, :, :, lanes].reshape(full).astype(F32)
        ids = pipe * (2 * HALF) + q * CHUNK + lax.broadcasted_iota(I32, full, 1)
        d = jnp.where(ids == twice(tcol[...]), twice(fcol[2]), e * twice(fcol[hh])).astype(BF16)
        cols = pl.ds(pl.multiple_of(q * CHUNK, CHUNK), CHUNK)
        dl[:, cols] = d
        acc[...] += jnp.dot(d, wm[cols, :], preferred_element_type=F32)

    bound = 0.51 * jnp.abs(fcol[2]) + 1e-6 * gcol[...]
    q16 = lanes_mul(acc[...], (TOP / bound).reshape(NB * ROWS, 128))
    q16 = jnp.round(jnp.clip(q16, -TOP, TOP)).astype(I32).astype(I16)
    dhs[...] = q16.reshape(NB, ROWS, CHUNK)

    @pl.loop(1, 16)
    def _(i):
        to = pipe_peer(i)
        send(dhs.at[to], dhr.at[pipe], d_send, d_recv, (me_dp, to))

    tn = (((0,), (0,)), ((), ()))

    @pl.loop(0, 2 * HALF // CHUNK)
    def _(q):
        cols = pl.ds(pl.multiple_of(q * CHUNK, CHUNK), CHUNK)
        x = lax.dot_general(dl[:, cols], hm[...].reshape(full), tn, preferred_element_type=F32)
        dwv[cols, :] = x.astype(BF16)
        pltpu.make_async_copy(dwv.at[cols], dw_ref.at[cols], dw_sem).start()

    dhr[pipe] = dhs[pipe]
    got15 = dhr.at[pl.ds(0, 15)]
    pltpu.make_async_copy(got15, got15, d_recv).wait()
    dh = jnp.sum(dhr[...].astype(I32).astype(F32), axis=0)
    own_bound = 0.51 * jnp.abs(fcol[2, pipe]) + 1e-6 * gcol[pipe]
    dh_ref[...] = lanes_mul(dh, own_bound * (1.0 / TOP)).astype(BF16)

    pltpu.make_async_copy(dwv, dw_ref, dw_sem).wait()
    for cp in pending:
        cp.wait_send()
    for cp in forwards:
        cp.wait_send()
    w_swap.wait_send()
    some = hm.at[pl.ds(0, 15)]
    pltpu.make_async_copy(some, some, h_send).wait()
    pltpu.make_async_copy(fifteen, fifteen, st_send.at[1]).wait()
    pltpu.make_async_copy(fifteen2, fifteen2, st_send.at[2]).wait()
    whole = e_all.at[c]
    pltpu.make_async_copy(whole, whole, ac_send).wait()
    pltpu.make_async_copy(got15, got15, d_send).wait()


def call(hidden, weight, targets, row_grad):
    dma = pltpu.SemaphoreType.DMA
    msg = (ROWS, SUB + CODE)
    vmem = pl.BlockSpec(memory_space=pltpu.VMEM)
    hbm = pl.BlockSpec(memory_space=pl.ANY)
    return pl.pallas_call(
        kernel,
        out_shape=(
            jax.ShapeDtypeStruct((ROWS, CHUNK), BF16),
            jax.ShapeDtypeStruct((2 * HALF, CHUNK), BF16),
            jax.ShapeDtypeStruct((2, 4), F32),
        ),
        in_specs=[vmem, hbm, vmem, vmem],
        out_specs=(vmem, hbm, vmem),
        scratch_shapes=[
            pltpu.VMEM((NB, ROWS, CHUNK), BF16),
            pltpu.VMEM((NB, ROWS, CHUNK), BF16),
            pltpu.VMEM((2 * HALF, CHUNK), BF16),
            pltpu.VMEM((HALF, CHUNK), BF16),
            pltpu.VMEM((NB, ROWS, HALF), F32),
            pltpu.VMEM((NB, ROWS, 128), F32),
            pltpu.VMEM((NB, ROWS, 128), I32),
            pltpu.VMEM((NB, ROWS, 128), F32),
            pltpu.VMEM((ROWS, HALF), F32),
            pltpu.VMEM((2, NSUB, NB, ROWS, SUB), BF16),
            pltpu.VMEM((NB * ROWS, 2 * HALF), BF16),
            pltpu.VMEM((2 * HALF, CHUNK), BF16),
            pltpu.VMEM((NB * ROWS, CHUNK), F32),
            pltpu.VMEM((3, NB, ROWS, 128), F32),
            pltpu.VMEM((8 * NSUB,) + msg, I16),
            pltpu.VMEM((8 * NSUB,) + msg, I16),
            pltpu.VMEM((4 * NSUB,) + msg, I16),
            pltpu.VMEM((4 * NSUB,) + msg, I16),
            pltpu.VMEM((3 * NSUB,) + msg, I16),
            pltpu.VMEM((3 * NSUB,) + msg, I16),
            pltpu.VMEM((1, 1, 384), F32),
            pltpu.VMEM((NB, 1, 384), F32),
            pltpu.VMEM((NB, 1, 384), F32),
            pltpu.VMEM((1, 1, 384), F32),
            pltpu.VMEM((NB, ROWS, CHUNK), I16),
            pltpu.VMEM((NB, ROWS, CHUNK), I16),
            dma, dma((2,)), dma, dma, dma((4,)), dma((4,)), dma((4,)),
            dma((8 * NSUB,)), dma((8 * NSUB,)), dma((4 * NSUB,)), dma((4 * NSUB,)), dma((3 * NSUB,)), dma((3 * NSUB,)),
            dma((3,)), dma((3,)),
            dma((8 * NSUB,)), dma((8 * NSUB,)), dma((4 * NSUB,)), dma((4 * NSUB,)), dma((3 * NSUB,)), dma((3 * NSUB,)),
            dma, dma, dma, dma, dma,
        ],
        compiler_params=pltpu.CompilerParams(
            collective_id=0, has_side_effects=True, vmem_limit_bytes=48 << 20
        ),
        cost_estimate=pl.CostEstimate(flops=1_600_000_000, bytes_accessed=5 << 20, transcendentals=1 << 20),
        name="output_layer",
    )(hidden, weight, targets, row_grad)


def on_device(hidden, weight, targets, row_grad):
    grad_hidden, grad_weight, row_loss = call(hidden.reshape(ROWS, CHUNK), weight, targets, row_grad)
    return grad_hidden.reshape(2, 8, CHUNK), grad_weight, row_loss


def solution(mesh):
    placed = (P(None, "pipe", "dp"), P("pipe", "dp"), P(), P())
    return jax.shard_map(
        on_device,
        mesh=mesh,
        in_specs=placed,
        out_specs=(P(None, "pipe", "dp"), P("pipe", "dp"), P(None, "dp")),
        check_vma=False,
    )
```

```python
import functools
import math

import jax
import jax.numpy as jnp
from jax import lax
from jax.experimental import pallas as pl
from jax.experimental.pallas import tpu as pltpu
from jax.sharding import PartitionSpec as P

MESH = pl.DeviceIdType.MESH
F32, BF16, I16, I32 = jnp.float32, jnp.bfloat16, jnp.int16, jnp.int32

Y, NB, ROWS = 8, 16, 16
HALF = 2048
SUB, NSUB = 1024, 2
CODE = 128
STEP = math.log(2.0) / 256
TOP = 32766.0
CHUNK = 256


def coords():
    dp, pipe = lax.axis_index("dp"), lax.axis_index("pipe")
    return dp // 4, (dp // 2) % 2, dp % 2, pipe


def lanes_mul(x, s):
    n = x.shape[1] // 128
    return jnp.concatenate([x[:, i * 128 : (i + 1) * 128] * s for i in range(n)], axis=1)


def encode(ref, slot, x, bound):
    code = jnp.ceil(jnp.log(jnp.maximum(bound, 1e-30)) * (1.0 / STEP)) + 1.0
    inv = TOP * jnp.exp(code * -STEP)
    ref[slot, :, :SUB] = jnp.round(lanes_mul(x, inv)).astype(I32).astype(I16)
    ref[slot, :, SUB:] = code.astype(I32).astype(I16)


def decode(ref, slot):
    scale = jnp.exp(ref[slot, :, SUB:].astype(I32).astype(F32) * STEP)
    x = ref[slot, :, :SUB].astype(I32).astype(F32)
    return lanes_mul(x, scale * (1.0 / TOP)), scale


def diagonal():
    return lax.broadcasted_iota(I32, (ROWS, 128), 0) == lax.broadcasted_iota(I32, (ROWS, 128), 1)


def to_lanes(col):
    return jnp.sum(jnp.where(diagonal(), col, 0.0), axis=0, keepdims=True)


def to_rows(row):
    shape = row.shape[:-2] + (ROWS, 128)
    at = len(shape) - 2
    eye = lax.broadcasted_iota(I32, shape, at) == lax.broadcasted_iota(I32, shape, at + 1)
    return jnp.broadcast_to(
        jnp.sum(jnp.where(eye, jnp.broadcast_to(row, shape), 0.0), axis=-1, keepdims=True), shape
    )


WAYS = ((4, 2), (3, 1), (-3, -1), (1, 1), (-1, -1), (2, 2), (-2, -2))
ORDER = (4, 3, -3, 2, -2, 1, -1, 0)
SIGNS = (1, -1)


def kernel(h_ref, w_ref, t_ref, g_ref, dh_ref, dw_ref, loss_ref, v, s):
    y, zl, c, pipe = coords()
    zh, px = pipe // 4, pipe % 4
    me_dp = y * 4 + zl * 2 + c
    mb = y * 2 + zl
    hm, hs, wm, ws, part, scale = v["hm"], v["hs"], v["wm"], v["ws"], v["part"], v["scale"]
    e_all, tcol, gcol, fcol, st1, st2 = v["e_all"], v["tcol"], v["gcol"], v["fcol"], v["st1"], v["st2"]

    def at_dp(yy, zz, cc):
        return (yy * 4 + zz * 2 + cc, pipe)

    def yo(o):
        return lax.rem(y + o + Y, Y)

    def block(o, zz):
        return yo(o) * 2 + zz

    def pipe_peer(i):
        return lax.rem(zh + i // 4, 4) * 4 + lax.rem(px + i % 4, 4)

    def dp_peer(i):
        return at_dp(lax.rem(y + i // 2, Y), lax.rem(zl + i % 2, 2), c)

    sib = at_dp(y, zl, 1 - c)
    zdev = at_dp(y, 1 - zl, c)
    pending = []

    def send(src, dst, s_sem, r_sem, dev):
        cp = pltpu.make_async_remote_copy(
            src_ref=src, dst_ref=dst, send_sem=s_sem, recv_sem=r_sem, device_id=dev, device_id_type=MESH
        )
        cp.start()
        return cp

    def push(src, dst, name, i, dev):
        cp = send(src, dst, s[name + "_s"].at[i], s[name + "_r"].at[i], dev)
        pending.append(cp)
        return cp

    def landed(ref, sem):
        pltpu.make_async_copy(ref, ref, sem).wait()

    local = [
        pltpu.make_async_copy(src, dst, s["local"].at[i])
        for i, (src, dst) in enumerate(((h_ref, hm.at[pipe]), (t_ref, v["t"]), (g_ref, v["g"]), (w_ref, wm)))
    ]
    for cp in local:
        cp.start()

    barrier = pltpu.get_barrier_semaphore()

    @pl.loop(1, 16)
    def _(i):
        pl.semaphore_signal(barrier, inc=1, device_id=(me_dp, pipe_peer(16 - i)), device_id_type=MESH)
        pl.semaphore_signal(barrier, inc=1, device_id=dp_peer(i), device_id_type=MESH)

    pl.semaphore_signal(barrier, inc=1, device_id=sib, device_id_type=MESH)
    for cp in local[:3]:
        cp.wait()
    pl.semaphore_wait(barrier, 31)

    @pl.loop(1, 16)
    def _(i):
        send(hm.at[pipe], hm.at[pipe], s["h_s"], s["h_r"].at[i // 4], (me_dp, pipe_peer(i)))

    half_rows = pl.ds(pl.multiple_of((1 - c) * HALF, HALF), HALF)
    w_swap = push(w_ref.at[half_rows], ws, "w", 0, sib)

    shape = (NB, ROWS, 128)
    b_id, r_id = lax.broadcasted_iota(I32, shape, 0), lax.broadcasted_iota(I32, shape, 1)
    pick = lax.broadcasted_iota(I32, shape, 2) == b_id * 8 + r_id % 8
    first = r_id < 8

    def column(ref):
        x = ref[...].astype(F32)
        x = jnp.where(first, x[0:1].reshape(1, 1, 128), x[1:2].reshape(1, 1, 128))
        return jnp.broadcast_to(jnp.sum(jnp.where(pick, x, 0.0), axis=-1, keepdims=True), shape)

    tcol[...] = column(v["t"]).astype(I32)
    gcol[...] = column(v["g"])

    full = (NB * ROWS, CHUNK)

    def twice(x):
        x = x.reshape(NB * ROWS, 128)
        return jnp.concatenate([x, x], axis=1)

    def at_target(q):
        ids = pipe * (2 * HALF) + q * CHUNK + lax.broadcasted_iota(I32, full, 1)
        return ids == twice(tcol[...])

    local[3].wait()
    v["wt"][...] = jnp.zeros(full, F32)

    @pl.loop(0, 2 * HALF // CHUNK)
    def _(q):
        cols = pl.ds(pl.multiple_of(q * CHUNK, CHUNK), CHUNK)
        one = jnp.where(at_target(q), 1.0, 0.0).astype(BF16)
        v["wt"][...] += jnp.dot(one, wm[cols, :], preferred_element_type=F32)

    near_first = (0, 1, 3, 2)
    forwards = []
    for n, dz in enumerate(near_first):
        group = pl.ds(lax.rem(zh + 4 - dz, 4) * 4, 4)
        landed(hm.at[pl.ds(0, 3 if dz == 0 else 4)], s["h_r"].at[dz])
        forwards.append(push(hm.at[group], hs.at[group], "hf", n, sib))
    for cp in forwards:
        cp.wait_recv()
    w_swap.wait_recv()

    nt = (((1,), (1,)), ((), ()))

    def products(u):
        scale[u] = jnp.zeros(shape, F32)

        @pl.loop(0, SUB // CHUNK)
        def _(k):
            k = u * (SUB // CHUNK) + k
            own = pl.ds(pl.multiple_of(c * HALF + k * CHUNK, CHUNK), CHUNK)
            there = pl.ds(pl.multiple_of(k * CHUNK, CHUNK), CHUNK)
            x = lax.dot_general(hm[...].reshape(full), wm[own, :], nt, preferred_element_type=F32)
            x += lax.dot_general(hs[...].reshape(full), ws[there, :], nt, preferred_element_type=F32)
            x = x.reshape(NB, ROWS, CHUNK)
            part[:, :, there] = x
            scale[u] = jnp.maximum(scale[u], jnp.maximum(jnp.abs(x[..., :128]), jnp.abs(x[..., 128:])))

        scale[u] = jnp.broadcast_to(jnp.max(scale[u], axis=-1, keepdims=True), shape)

    def lanes(u):
        return slice(u * SUB, (u + 1) * SUB)

    z_way = {}

    def z_issue():
        for n, o in enumerate(ORDER):
            b = block(o * SIGNS[0], 1 - zl)
            encode(v["zs"], n, part[b, :, lanes(0)], scale[0, b])
            z_way[o] = push(v["zs"].at[n], v["zr"].at[n], "z", n, zdev)

    def get(u, o):
        if u == 0:
            b = block(o * SIGNS[0], zl)
            z_way[o].wait_recv()
            x, bound = decode(v["zr"], ORDER.index(o))
            return part[b, :, lanes(0)] + x, scale[0, b] + bound
        pair = pl.ds(block(o * SIGNS[1], 0), 2)
        return part[pair, :, lanes(1)].reshape(2 * ROWS, SUB), scale[1, pair].reshape(2 * ROWS, 128)

    y_way = {}

    def add(u, got, *slots):
        x, bound = got
        for i in slots:
            y_way[u, i].wait_recv()
            more, more_bound = decode(v[f"yr{u}"], i)
            x, bound = x + more, bound + more_bound
        return x, bound

    def y_push(u, i, got):
        encode(v[f"ys{u}"], i, *got)
        dev = at_dp(yo(SIGNS[u] * WAYS[i][1]), zl, c)
        y_way[u, i] = push(v[f"ys{u}"].at[i], v[f"yr{u}"].at[i], f"y{u}", i, dev)

    def rs_first(u):
        for i in (0, 1, 2):
            y_push(u, i, get(u, WAYS[i][0]))

    def rs_near(u):
        for i in (3, 4):
            y_push(u, i, get(u, WAYS[i][0]))

    def rs_mid(u):
        y_push(u, 5, add(u, get(u, 2), 0, 1))
        y_push(u, 6, add(u, get(u, -2), 2))

    def rs_end(u):
        return add(u, get(u, 0), 3, 4, 5, 6)

    def rs_pair():
        x, bound = rs_end(1)
        v["xb"][...] = x.reshape(2, ROWS, SUB)
        v["sb"][...] = bound.reshape(2, ROWS, 128)
        encode(v["zs"], 8, v["xb"][1 - zl], v["sb"][1 - zl])
        z_way["pair"] = push(v["zs"].at[8], v["zr"].at[8], "z", 8, zdev)

    def rs_pair_end():
        z_way["pair"].wait_recv()
        return v["xb"][zl] + decode(v["zr"], 8)[0]

    wide = (ROWS, 128)

    def softmax(u, x):
        m_col = jnp.max(x, axis=1, keepdims=True)
        e = jnp.exp(x - m_col)
        s_col = jnp.sum(e, axis=1, keepdims=True)
        ids = pipe * (2 * HALF) + c * HALF + u * SUB + lax.broadcasted_iota(I32, x.shape, 1)
        hit = ids == jnp.concatenate([tcol[mb]] * (SUB // 128), axis=1)
        p_col = jnp.sum(jnp.where(hit, x, 0.0), axis=1, keepdims=True)
        e_all[c, u, mb] = jnp.where(hit, 0.0, e).astype(BF16)
        return [to_lanes(jnp.broadcast_to(a, wide)) for a in (m_col, s_col, p_col)]

    def chunk(u, b):
        return e_all.at[c, u, b]

    def ag_y(u, i, o, hop):
        b = block(o * SIGNS[u], zl)
        push(chunk(u, b), chunk(u, b), f"ay{u}", i, at_dp(yo(SIGNS[u] * hop), zl, c))

    def to_core(u, b):
        send(chunk(u, b), chunk(u, b), s["ac_s"], s["ac_r"].at[u], sib)

    def share(u, o):
        b = block(o * SIGNS[u], zl)
        push(chunk(u, b), chunk(u, b), f"az{u}", ORDER.index(o), zdev)
        to_core(u, b)

    def got_y(u, i, o):
        landed(chunk(u, block(o * SIGNS[u], zl)), s[f"ay{u}_r"].at[i])

    def got_z(u, *offsets):
        for o in offsets:
            b = block(o * SIGNS[u], 1 - zl)
            landed(chunk(u, b), s[f"az{u}_r"].at[ORDER.index(o)])
            to_core(u, b)

    def ag_own(u):
        for i, hop in ((1, 2), (3, -2), (0, 1), (2, -1)):
            ag_y(u, i, 0, hop)
        share(u, 0)

    def ag_near(u):
        got_y(u, 0, -1)
        share(u, -1)
        got_y(u, 2, 1)
        share(u, 1)
        got_y(u, 1, -2)
        ag_y(u, 5, -2, 2)
        ag_y(u, 4, -2, 1)
        share(u, -2)
        got_y(u, 3, 2)
        ag_y(u, 6, 2, -1)
        share(u, 2)

    def ag_far(u):
        for i, o in ((4, -3), (6, 3), (5, 4)):
            got_y(u, i, o)
            share(u, o)

    def weigh(u):
        landed(e_all.at[1 - c, u], s["ac_r"].at[u])
        for half in range(2):
            rows = slice(half * HALF + u * SUB, half * HALF + (u + 1) * SUB)
            e = e_all[half, u].reshape(NB * ROWS, SUB)
            v["acc"][half * 2 + u] = jnp.dot(e, wm[rows, :], preferred_element_type=F32)

    products(0)
    z_issue()
    products(1)
    rs_first(1)
    rs_near(1)
    rs_first(0)
    rs_near(0)
    rs_mid(1)
    rs_mid(0)
    rs_pair()
    stats0 = softmax(0, rs_end(0)[0])
    ag_own(0)
    stats1 = softmax(1, rs_pair_end())
    ag_own(1)

    def put(ref, rows):
        for n, row in enumerate(rows):
            ref[:, n * 128 : (n + 1) * 128] = row

    m_own = jnp.maximum(stats0[0], stats1[0])
    s_own = stats0[1] * jnp.exp(stats0[0] - m_own) + stats1[1] * jnp.exp(stats1[0] - m_own)
    put(v["mine"].at[0], (m_own, s_own, stats0[2] + stats1[2], stats0[0], stats1[0]))
    both = push(v["mine"].at[0], v["st0"].at[0], "st0", 0, sib)
    ag_near(0)
    both.wait_recv()
    other = [v["st0"][0, :, n * 128 : (n + 1) * 128] for n in range(5)]
    m_two = jnp.maximum(m_own, other[0])
    s_two = s_own * jnp.exp(m_own - m_two) + other[1] * jnp.exp(other[0] - m_two)
    put(st1.at[pipe], (m_two, s_two, stats0[2] + stats1[2] + other[2]))

    @pl.loop(1, 16)
    def _(i):
        send(st1.at[pipe], st1.at[pipe], s["st_s"].at[0], s["st_r"].at[0], (me_dp, pipe_peer(i)))

    ag_near(1)
    got_z(0, 0)
    ag_far(0)
    got_z(0, -1, 1)
    got_z(1, 0)
    ag_far(1)

    fifteen = st1.at[pl.ds(0, 15)]
    landed(fifteen, s["st_r"].at[0])
    ms, sums, picks = (st1[:, 0, n * 128 : (n + 1) * 128] for n in range(3))
    top = jnp.max(ms, axis=0, keepdims=True)
    total = jnp.sum(sums * jnp.exp(ms - top), axis=0, keepdims=True)
    picked = jnp.sum(picks, axis=0, keepdims=True)
    total = jnp.where(lax.broadcasted_iota(I32, (1, 128), 1) < ROWS, total, 1.0)
    g = to_lanes(gcol[mb])
    f_own = [g * (jnp.exp(st[0] - top) / total) for st in (stats0, stats1)]
    f_other = [g * (jnp.exp(m - top) / total) for m in other[3:]]
    at_hit = g * (jnp.exp(picked - top) / total - 1.0)
    loss = top + jnp.log(total) - picked
    low = [jnp.where(c == 0, a, b) for a, b in zip(f_own, f_other)]
    high = [jnp.where(c == 0, b, a) for a, b in zip(f_own, f_other)]
    put(st2.at[mb], (*low, *high, at_hit))

    @pl.loop(1, 16)
    def _(i):
        send(st2.at[mb], st2.at[mb], s["st_s"].at[1], s["st_r"].at[1], dp_peer(i))

    got_z(0, -2, 2)
    got_z(0, -3, 3, 4)
    got_z(1, -1, 1, -2, 2)
    weigh(0)
    loss_col = to_rows(loss)
    r2, l2 = lax.broadcasted_iota(I32, wide, 0), lax.broadcasted_iota(I32, wide, 1)
    loss_out = jnp.where(r2 % 8 == 4 * c + l2, loss_col, 0.0).reshape(2, 8, 128)
    v["loss"][...] = jnp.sum(loss_out, axis=1)
    got_z(1, -3, 3, 4)
    fifteen2 = st2.at[pl.ds(0, 15)]
    landed(fifteen2, s["st_r"].at[1])
    for n in range(5):
        fcol[n] = to_rows(st2[:, :, n * 128 : (n + 1) * 128])
    weigh(1)

    bound = 0.51 * jnp.abs(fcol[4]) + 1e-6 * gcol[...]
    dh = v["wt"][...] * twice(fcol[4])
    for n in range(4):
        dh += v["acc"][n] * twice(fcol[n])
    q16 = jnp.clip(dh * twice(TOP / bound), -TOP, TOP)
    v["dhs"][...] = jnp.round(q16).astype(I32).astype(I16).reshape(NB, ROWS, CHUNK)

    @pl.loop(1, 16)
    def _(i):
        to = pipe_peer(i)
        send(v["dhs"].at[to], v["dhr"].at[pipe], s["d_s"], s["d_r"], (me_dp, to))

    tn = (((0,), (0,)), ((), ()))

    @pl.loop(0, 2 * HALF // CHUNK)
    def _(q):
        hh, u, k = q // 8, (q // 4) % 2, q % 4
        e = e_all[hh, u, :, :, pl.ds(pl.multiple_of(k * CHUNK, CHUNK), CHUNK)].reshape(full).astype(F32)
        d = jnp.where(at_target(q), twice(fcol[4]), e * twice(fcol[hh * 2 + u])).astype(BF16)
        x = lax.dot_general(d, hm[...].reshape(full), tn, preferred_element_type=F32)
        rows = pl.ds(pl.multiple_of(q * CHUNK, CHUNK), CHUNK)
        v["dw"][rows, :] = x.astype(BF16)
        pltpu.make_async_copy(v["dw"].at[rows], dw_ref.at[rows], s["dw"]).start()

    v["dhr"][pipe] = v["dhs"][pipe]
    got15 = v["dhr"].at[pl.ds(0, 15)]
    landed(got15, s["d_r"])
    dh = jnp.sum(v["dhr"][...].astype(I32).astype(F32), axis=0)
    own_bound = 0.51 * jnp.abs(fcol[4, pipe]) + 1e-6 * gcol[pipe]
    v["dh"][...] = lanes_mul(dh, own_bound * (1.0 / TOP)).astype(BF16)
    outs = [
        pltpu.make_async_copy(src, dst, s["local"].at[i])
        for i, (src, dst) in enumerate(((v["dh"], dh_ref), (v["loss"], loss_ref)))
    ]
    for cp in outs:
        cp.start()

    for cp in pending:
        cp.wait_send()
    landed(hm.at[pl.ds(0, 15)], s["h_s"])
    landed(fifteen, s["st_s"].at[0])
    landed(fifteen2, s["st_s"].at[1])
    landed(e_all.at[c], s["ac_s"])
    landed(got15, s["d_s"])
    pltpu.make_async_copy(v["dw"], dw_ref, s["dw"]).wait()
    for cp in outs:
        cp.wait()


def call(hidden, weight, targets, row_grad):
    dma, vm = pltpu.SemaphoreType.DMA, pltpu.VMEM
    one, two = (ROWS, SUB + CODE), (2 * ROWS, SUB + CODE)
    hbm = pl.BlockSpec(memory_space=pltpu.HBM)
    buffers = dict(
        hm=vm((NB, ROWS, CHUNK), BF16), hs=vm((NB, ROWS, CHUNK), BF16),
        wm=vm((2 * HALF, CHUNK), BF16), ws=vm((HALF, CHUNK), BF16),
        part=vm((NB, ROWS, HALF), F32), scale=vm((NSUB, NB, ROWS, 128), F32),
        t=vm((2, 128), I32), g=vm((2, 128), F32), tcol=vm((NB, ROWS, 128), I32), gcol=vm((NB, ROWS, 128), F32),
        wt=vm((NB * ROWS, CHUNK), F32), acc=vm((4, NB * ROWS, CHUNK), F32), fcol=vm((5, NB, ROWS, 128), F32),
        e_all=vm((2, NSUB, NB, ROWS, SUB), BF16), dw=vm((2 * HALF, CHUNK), BF16),
        zs=vm((9,) + one, I16), zr=vm((9,) + one, I16), ys0=vm((7,) + one, I16), yr0=vm((7,) + one, I16),
        ys1=vm((7,) + two, I16), yr1=vm((7,) + two, I16), xb=vm((2, ROWS, SUB), F32), sb=vm((2, ROWS, 128), F32),
        mine=vm((1, 1, 640), F32), st0=vm((1, 1, 640), F32), st1=vm((NB, 1, 384), F32), st2=vm((NB, 1, 640), F32),
        dhs=vm((NB, ROWS, CHUNK), I16), dhr=vm((NB, ROWS, CHUNK), I16), dh=vm((ROWS, CHUNK), BF16),
        loss=vm((2, 128), F32),
    )
    pairs = dict(w=1, hf=4, z=9, y0=7, y1=7, ay0=7, ay1=7, az0=8, az1=8, st0=1, st=2)
    sems = dict(
        local=dma((4,)), h_s=dma, h_r=dma((4,)), ac_s=dma, ac_r=dma((2,)), d_s=dma, d_r=dma, dw=dma,
        **{name + end: dma((n,)) for name, n in pairs.items() for end in ("_s", "_r")},
    )
    return pl.pallas_call(
        kernel,
        out_shape=(
            jax.ShapeDtypeStruct((ROWS, CHUNK), BF16),
            jax.ShapeDtypeStruct((2 * HALF, CHUNK), BF16),
            jax.ShapeDtypeStruct((2, 128), F32),
        ),
        in_specs=[hbm] * 4,
        out_specs=(hbm,) * 3,
        scratch_shapes=(buffers, sems),
        compiler_params=pltpu.CompilerParams(
            collective_id=0, has_side_effects=True, vmem_limit_bytes=60 << 20
        ),
        cost_estimate=pl.CostEstimate(flops=1_600_000_000, bytes_accessed=5 << 20, transcendentals=1 << 20),
        name="output_layer",
    )(hidden, weight, targets, row_grad)


PIECES = 8


def settle(dh, dw, loss, dh_out, dw_out, loss_out, dh_v, dw_v, loss_v, sem_in, sem_out):
    rows = 2 * HALF // PIECES
    moves = [(dh, dh_v, dh_out), (loss, loss_v, loss_out)]
    for i in range(PIECES):
        at = pl.ds(i * rows, rows)
        moves.append((dw.at[at], dw_v.at[at], dw_out.at[at]))
    into = [pltpu.make_async_copy(a, b, sem_in.at[i]) for i, (a, b, _) in enumerate(moves)]
    out = [pltpu.make_async_copy(b, d, sem_out.at[i]) for i, (_, b, d) in enumerate(moves)]
    for cp in into:
        cp.start()
    for cp, then in zip(into, out):
        cp.wait()
        then.start()
    for cp in out:
        cp.wait()


def on_device(hidden, weight, targets, row_grad):
    found = call(hidden.reshape(ROWS, CHUNK), weight, targets, row_grad)
    hbm = pl.BlockSpec(memory_space=pltpu.HBM)
    grad_hidden, grad_weight, row_loss = pl.pallas_call(
        settle,
        out_shape=[jax.ShapeDtypeStruct(x.shape, x.dtype) for x in found],
        in_specs=[hbm] * 3,
        out_specs=[hbm] * 3,
        scratch_shapes=[pltpu.VMEM(x.shape, x.dtype) for x in found]
        + [pltpu.SemaphoreType.DMA((PIECES + 2,)), pltpu.SemaphoreType.DMA((PIECES + 2,))],
        compiler_params=pltpu.CompilerParams(vmem_limit_bytes=60 << 20),
        name="settle",
    )(*found)
    return grad_hidden.reshape(2, 8, CHUNK), grad_weight, row_loss[:, :4]


def solution(mesh):
    placed = (P(None, "pipe", "dp"), P("pipe", "dp"), P(), P())
    return jax.shard_map(
        on_device,
        mesh=mesh,
        in_specs=placed,
        out_specs=(P(None, "pipe", "dp"), P("pipe", "dp"), P(None, "dp")),
        check_vma=False,
    )
```

```python
import functools
import math

import jax
import jax.numpy as jnp
from jax import lax
from jax.experimental import pallas as pl
from jax.experimental.pallas import tpu as pltpu
from jax.sharding import PartitionSpec as P

MESH = pl.DeviceIdType.MESH
F32, BF16, I16, I32 = jnp.float32, jnp.bfloat16, jnp.int16, jnp.int32

Y, NB, ROWS = 8, 16, 16
HALF = 2048
SUB, NSUB = 1024, 2
CODE = 128
STEP = math.log(2.0) / 256
TOP = 32766.0
CHUNK = 256


def coords():
    dp, pipe = lax.axis_index("dp"), lax.axis_index("pipe")
    return dp // 4, (dp // 2) % 2, dp % 2, pipe


def lanes_mul(x, s):
    n = x.shape[1] // 128
    return jnp.concatenate([x[:, i * 128 : (i + 1) * 128] * s for i in range(n)], axis=1)


def encode(ref, slot, x, bound):
    code = jnp.ceil(jnp.log(jnp.maximum(bound, 1e-30)) * (1.0 / STEP)) + 1.0
    inv = TOP * jnp.exp(code * -STEP)
    ref[slot, :, :SUB] = jnp.round(lanes_mul(x, inv)).astype(I32).astype(I16)
    ref[slot, :, SUB:] = code.astype(I32).astype(I16)


def decode(ref, slot):
    scale = jnp.exp(ref[slot, :, SUB:].astype(I32).astype(F32) * STEP)
    x = ref[slot, :, :SUB].astype(I32).astype(F32)
    return lanes_mul(x, scale * (1.0 / TOP)), scale


def diagonal():
    return lax.broadcasted_iota(I32, (ROWS, 128), 0) == lax.broadcasted_iota(I32, (ROWS, 128), 1)


def to_lanes(col):
    return jnp.sum(jnp.where(diagonal(), col, 0.0), axis=0, keepdims=True)


def to_rows(row):
    shape = row.shape[:-2] + (ROWS, 128)
    at = len(shape) - 2
    eye = lax.broadcasted_iota(I32, shape, at) == lax.broadcasted_iota(I32, shape, at + 1)
    return jnp.broadcast_to(
        jnp.sum(jnp.where(eye, jnp.broadcast_to(row, shape), 0.0), axis=-1, keepdims=True), shape
    )


WAYS = ((4, 2), (3, 1), (-3, -1), (1, 1), (-1, -1), (2, 2), (-2, -2))
CROSS = (4, 3, -3, 2, -2, 0)
WIDTHS = dict(z=6, x=2, y=7)
SIGNS = (1, -1)


def kernel(h_ref, w_ref, t_ref, g_ref, dh_ref, dw_ref, loss_ref, v, s):
    y, zl, c, pipe = coords()
    zh, px = pipe // 4, pipe % 4
    me_dp = y * 4 + zl * 2 + c
    mb = y * 2 + zl
    hm, hs, wm, ws, part, scale = v["hm"], v["hs"], v["wm"], v["ws"], v["part"], v["scale"]
    e_all, tcol, gcol, fcol, st1, st2 = v["e_all"], v["tcol"], v["gcol"], v["fcol"], v["st1"], v["st2"]

    def at_dp(yy, zz, cc):
        return (yy * 4 + zz * 2 + cc, pipe)

    def yo(o):
        return lax.rem(y + o + Y, Y)

    def block(o, zz):
        return yo(o) * 2 + zz

    def far_first(j):
        return lax.rem(j + 7, 15) + 1

    def pipe_peer(i):
        return lax.rem(zh + i // 4, 4) * 4 + lax.rem(px + i % 4, 4)

    def dp_peer(i):
        return at_dp(lax.rem(y + i // 2, Y), lax.rem(zl + i % 2, 2), c)

    sib = at_dp(y, zl, 1 - c)
    zdev = at_dp(y, 1 - zl, c)
    pending = []

    def send(src, dst, s_sem, r_sem, dev):
        cp = pltpu.make_async_remote_copy(
            src_ref=src, dst_ref=dst, send_sem=s_sem, recv_sem=r_sem, device_id=dev, device_id_type=MESH
        )
        cp.start()
        return cp

    def push(src, dst, name, i, dev):
        cp = send(src, dst, s[name + "_s"].at[i], s[name + "_r"].at[i], dev)
        pending.append(cp)
        return cp

    def landed(ref, sem):
        pltpu.make_async_copy(ref, ref, sem).wait()

    local = [
        pltpu.make_async_copy(src, dst, s["local"].at[i])
        for i, (src, dst) in enumerate(((h_ref, hm.at[pipe]), (t_ref, v["t"]), (g_ref, v["g"]), (w_ref, wm)))
    ]
    for cp in local:
        cp.start()

    barrier = pltpu.get_barrier_semaphore()

    @pl.loop(0, 15)
    def _(j):
        i = far_first(j)
        pl.semaphore_signal(barrier, inc=1, device_id=(me_dp, pipe_peer(i)), device_id_type=MESH)
        pl.semaphore_signal(barrier, inc=1, device_id=dp_peer(i), device_id_type=MESH)

    pl.semaphore_signal(barrier, inc=1, device_id=sib, device_id_type=MESH)
    for cp in local[:3]:
        cp.wait()
    pl.semaphore_wait(barrier, 31)

    @pl.loop(0, 15)
    def _(j):
        i = far_first(j)
        send(hm.at[pipe], hm.at[pipe], s["h_s"], s["h_r"].at[i // 4], (me_dp, pipe_peer(i)))

    half_rows = pl.ds(pl.multiple_of((1 - c) * HALF, HALF), HALF)
    w_swap = push(w_ref.at[half_rows], ws, "w", 0, sib)

    shape = (NB, ROWS, 128)
    b_id, r_id = lax.broadcasted_iota(I32, shape, 0), lax.broadcasted_iota(I32, shape, 1)
    pick = lax.broadcasted_iota(I32, shape, 2) == b_id * 8 + r_id % 8
    first = r_id < 8

    def column(ref):
        x = ref[...].astype(F32)
        x = jnp.where(first, x[0:1].reshape(1, 1, 128), x[1:2].reshape(1, 1, 128))
        return jnp.broadcast_to(jnp.sum(jnp.where(pick, x, 0.0), axis=-1, keepdims=True), shape)

    tcol[...] = column(v["t"]).astype(I32)
    gcol[...] = column(v["g"])

    full = (NB * ROWS, CHUNK)

    def twice(x):
        x = x.reshape(NB * ROWS, 128)
        return jnp.concatenate([x, x], axis=1)

    def at_target(q):
        ids = pipe * (2 * HALF) + q * CHUNK + lax.broadcasted_iota(I32, full, 1)
        return ids == twice(tcol[...])

    local[3].wait()
    v["wt"][...] = jnp.zeros(full, F32)

    @pl.loop(0, 2 * HALF // CHUNK)
    def _(q):
        cols = pl.ds(pl.multiple_of(q * CHUNK, CHUNK), CHUNK)
        one = jnp.where(at_target(q), 1.0, 0.0).astype(BF16)
        v["wt"][...] += jnp.dot(one, wm[cols, :], preferred_element_type=F32)

    near_first = (0, 1, 3, 2)
    forwards = []
    for n, dz in enumerate(near_first):
        group = pl.ds(lax.rem(zh + 4 - dz, 4) * 4, 4)
        landed(hm.at[pl.ds(0, 3 if dz == 0 else 4)], s["h_r"].at[dz])
        forwards.append(push(hm.at[group], hs.at[group], "hf", n, sib))
    for cp in forwards:
        cp.wait_recv()
    w_swap.wait_recv()

    nt = (((1,), (1,)), ((), ()))

    def products(u):
        scale[u] = jnp.zeros(shape, F32)

        for k in range(u * SUB // CHUNK, (u + 1) * SUB // CHUNK):
            own = pl.ds(pl.multiple_of(c * HALF + k * CHUNK, CHUNK), CHUNK)
            there = pl.ds(k * CHUNK, CHUNK)
            x = lax.dot_general(hm[...].reshape(full), wm[own, :], nt, preferred_element_type=F32)
            x += lax.dot_general(hs[...].reshape(full), ws[there, :], nt, preferred_element_type=F32)
            x = x.reshape(NB, ROWS, CHUNK)
            part[:, :, there] = x
            scale[u] = jnp.maximum(scale[u], jnp.maximum(jnp.abs(x[..., :128]), jnp.abs(x[..., 128:])))

        scale[u] = jnp.broadcast_to(jnp.max(scale[u], axis=-1, keepdims=True), shape)

    def lanes(u):
        return slice(u * SUB, (u + 1) * SUB)

    def own(u, b):
        return part[b, :, lanes(u)], scale[u, b]

    way = {}

    def go(u, name, i, got, dev):
        encode(v[f"{name}s"], u * WIDTHS[name] + i, *got)
        slot = u * WIDTHS[name] + i
        way[name, u, i] = push(v[f"{name}s"].at[slot], v[f"{name}r"].at[slot], name, slot, dev)

    def add(u, got, name, *slots):
        x, bound = got
        for i in slots:
            way[name, u, i].wait_recv()
            more, more_bound = decode(v[f"{name}r"], u * WIDTHS[name] + i)
            x, bound = x + more, bound + more_bound
        return x, bound

    def at_y(u, hop):
        return at_dp(yo(SIGNS[u] * hop), zl, c)

    def rs_z(u, *offsets):
        for o in offsets:
            go(u, "z", CROSS.index(o), own(u, block(o * SIGNS[u], 1 - zl)), zdev)

    def rs_side(u):
        for i, o in enumerate((1, -1)):
            go(u, "x", i, own(u, block(o * SIGNS[u], 1 - zl)), at_y(u, o))

    def rs_near(u):
        for i in (3, 4):
            o, hop = WAYS[i]
            go(u, "y", i, own(u, block(o * SIGNS[u], zl)), at_y(u, hop))

    def rs_z_own(u):
        go(u, "z", 5, add(u, own(u, block(0, 1 - zl)), "x", 0, 1), zdev)

    def crossed(u, o):
        return add(u, own(u, block(o * SIGNS[u], zl)), "z", CROSS.index(o))

    def rs_first(u):
        for i in (0, 1, 2):
            go(u, "y", i, crossed(u, WAYS[i][0]), at_y(u, WAYS[i][1]))

    def rs_mid(u):
        go(u, "y", 5, add(u, crossed(u, 2), "y", 0, 1), at_y(u, 2))
        go(u, "y", 6, add(u, crossed(u, -2), "y", 2), at_y(u, -2))

    def rs_end(u):
        return add(u, crossed(u, 0), "y", 3, 4, 5, 6)[0]

    wide = (ROWS, 128)

    def softmax(u, x):
        m_col = jnp.max(x, axis=1, keepdims=True)
        e = jnp.exp(x - m_col)
        s_col = jnp.sum(e, axis=1, keepdims=True)
        ids = pipe * (2 * HALF) + c * HALF + u * SUB + lax.broadcasted_iota(I32, x.shape, 1)
        hit = ids == jnp.concatenate([tcol[mb]] * (SUB // 128), axis=1)
        p_col = jnp.sum(jnp.where(hit, x, 0.0), axis=1, keepdims=True)
        e_all[c, u, mb] = jnp.where(hit, 0.0, e).astype(BF16)
        return [to_lanes(jnp.broadcast_to(a, wide)) for a in (m_col, s_col, p_col)]

    def chunk(u, o, side=0):
        return e_all.at[c, u, block(o * SIGNS[u], zl if side == 0 else 1 - zl)]

    def to_core(u, ref):
        send(ref, ref, s["ac_s"], s["ac_r"].at[u], sib)

    def ag(u, name, i, ref, dev):
        push(ref, ref, "a" + name, u * WIDTHS[name] + i, dev)

    def got(u, name, i, ref):
        landed(ref, s[f"a{name}_r"].at[u * WIDTHS[name] + i])

    def cross(u, o):
        ag(u, "z", CROSS.index(o), chunk(u, o), zdev)

    def ag_own(u):
        ref = chunk(u, 0)
        cross(u, 0)
        for i, hop in ((1, 2), (3, -2), (0, 1), (2, -1)):
            ag(u, "y", i, ref, at_y(u, hop))
        to_core(u, ref)

    def ag_side(u):
        ref = chunk(u, 0, 1)
        got(u, "z", 5, ref)
        for i, hop in enumerate((1, -1)):
            ag(u, "x", i, ref, at_y(u, hop))
        to_core(u, ref)

    def ag_near(u):
        got(u, "y", 1, chunk(u, -2))
        ag(u, "y", 5, chunk(u, -2), at_y(u, 2))
        ag(u, "y", 4, chunk(u, -2), at_y(u, 1))
        cross(u, -2)
        got(u, "y", 3, chunk(u, 2))
        ag(u, "y", 6, chunk(u, 2), at_y(u, -1))
        cross(u, 2)
        for i, o in ((0, -1), (2, 1)):
            got(u, "y", i, chunk(u, o))
        for o in (-2, 2, -1, 1):
            to_core(u, chunk(u, o))

    def ag_far(u):
        for i, o in ((4, -3), (6, 3), (5, 4)):
            got(u, "y", i, chunk(u, o))
            cross(u, o)
            to_core(u, chunk(u, o))

    def ag_side_near(u):
        for i, o in enumerate((-1, 1)):
            got(u, "x", i, chunk(u, o, 1))
            to_core(u, chunk(u, o, 1))

    def ag_crossed(u, *offsets):
        for o in offsets:
            got(u, "z", CROSS.index(o), chunk(u, o, 1))
            to_core(u, chunk(u, o, 1))

    def weigh(u):
        landed(e_all.at[1 - c, u], s["ac_r"].at[u])
        for half in range(2):
            rows = slice(half * HALF + u * SUB, half * HALF + (u + 1) * SUB)
            e = e_all[half, u].reshape(NB * ROWS, SUB)
            v["acc"][half * 2 + u] = jnp.dot(e, wm[rows, :], preferred_element_type=F32)

    products(0)
    rs_z(0, 4, 3, -3)
    rs_side(0)
    products(1)
    rs_z(1, 4, 3, -3)
    rs_side(1)
    rs_z(0, 2, -2)
    rs_z(1, 2, -2)
    rs_first(0)
    rs_near(0)
    rs_z_own(0)
    rs_first(1)
    rs_near(1)
    rs_z_own(1)
    rs_mid(0)
    rs_mid(1)
    stats0 = softmax(0, rs_end(0))
    ag_own(0)
    stats1 = softmax(1, rs_end(1))
    ag_own(1)

    def put(ref, rows):
        for n, row in enumerate(rows):
            ref[:, n * 128 : (n + 1) * 128] = row

    m_own = jnp.maximum(stats0[0], stats1[0])
    s_own = stats0[1] * jnp.exp(stats0[0] - m_own) + stats1[1] * jnp.exp(stats1[0] - m_own)
    put(v["mine"].at[0], (m_own, s_own, stats0[2] + stats1[2], stats0[0], stats1[0]))
    both = push(v["mine"].at[0], v["st0"].at[0], "st0", 0, sib)
    ag_side(0)
    both.wait_recv()
    other = [v["st0"][0, :, n * 128 : (n + 1) * 128] for n in range(5)]
    m_two = jnp.maximum(m_own, other[0])
    s_two = s_own * jnp.exp(m_own - m_two) + other[1] * jnp.exp(other[0] - m_two)
    put(st1.at[pipe], (m_two, s_two, stats0[2] + stats1[2] + other[2]))

    @pl.loop(0, 15)
    def _(j):
        i = far_first(j)
        send(st1.at[pipe], st1.at[pipe], s["st_s"].at[0], s["st_r"].at[0], (me_dp, pipe_peer(i)))

    ag_near(0)
    ag_side(1)
    ag_near(1)
    ag_side_near(0)
    ag_far(0)
    ag_side_near(1)
    ag_far(1)

    fifteen = st1.at[pl.ds(0, 15)]
    landed(fifteen, s["st_r"].at[0])
    ms, sums, picks = (st1[:, 0, n * 128 : (n + 1) * 128] for n in range(3))
    top = jnp.max(ms, axis=0, keepdims=True)
    total = jnp.sum(sums * jnp.exp(ms - top), axis=0, keepdims=True)
    picked = jnp.sum(picks, axis=0, keepdims=True)
    total = jnp.where(lax.broadcasted_iota(I32, (1, 128), 1) < ROWS, total, 1.0)
    g = to_lanes(gcol[mb])
    f_own = [g * (jnp.exp(st[0] - top) / total) for st in (stats0, stats1)]
    f_other = [g * (jnp.exp(m - top) / total) for m in other[3:]]
    at_hit = g * (jnp.exp(picked - top) / total - 1.0)
    loss = top + jnp.log(total) - picked
    low = [jnp.where(c == 0, a, b) for a, b in zip(f_own, f_other)]
    high = [jnp.where(c == 0, b, a) for a, b in zip(f_own, f_other)]
    put(st2.at[mb], (*low, *high, at_hit.astype(BF16).astype(F32)))

    @pl.loop(0, 15)
    def _(j):
        i = far_first(j)
        send(st2.at[mb], st2.at[mb], s["st_s"].at[1], s["st_r"].at[1], dp_peer(i))

    ag_crossed(0, -2, 2)
    ag_crossed(1, -2, 2)
    ag_crossed(0, -3, 3, 4)
    weigh(0)
    loss_col = to_rows(loss)
    r2, l2 = lax.broadcasted_iota(I32, wide, 0), lax.broadcasted_iota(I32, wide, 1)
    loss_out = jnp.where(r2 % 8 == 4 * c + l2, loss_col, 0.0).reshape(2, 8, 128)
    v["loss"][...] = jnp.sum(loss_out, axis=1)
    ag_crossed(1, -3, 3, 4)
    fifteen2 = st2.at[pl.ds(0, 15)]
    landed(fifteen2, s["st_r"].at[1])
    for n in range(5):
        fcol[n] = to_rows(st2[:, :, n * 128 : (n + 1) * 128])
    weigh(1)

    bound = 0.51 * jnp.abs(fcol[4]) + 1e-6 * gcol[...]
    dh = v["wt"][...] * twice(fcol[4])
    for n in range(4):
        dh += v["acc"][n] * twice(fcol[n])
    q16 = jnp.clip(dh * twice(TOP / bound), -TOP, TOP)
    v["dhs"][...] = jnp.round(q16).astype(I32).astype(I16).reshape(NB, ROWS, CHUNK)

    @pl.loop(0, 15)
    def _(j):
        i = far_first(j)
        to = pipe_peer(i)
        send(v["dhs"].at[to], v["dhr"].at[pipe], s["d_s"], s["d_r"], (me_dp, to))

    tn = (((0,), (0,)), ((), ()))

    @pl.loop(0, 2 * HALF // CHUNK)
    def _(q):
        hh, u, k = q // 8, (q // 4) % 2, q % 4
        e = e_all[hh, u, :, :, pl.ds(pl.multiple_of(k * CHUNK, CHUNK), CHUNK)].reshape(full).astype(F32)
        d = jnp.where(at_target(q), twice(fcol[4]), e * twice(fcol[hh * 2 + u])).astype(BF16)
        x = lax.dot_general(d, hm[...].reshape(full), tn, preferred_element_type=F32)
        rows = pl.ds(pl.multiple_of(q * CHUNK, CHUNK), CHUNK)
        v["dw"][rows, :] = x.astype(BF16)
        pltpu.make_async_copy(v["dw"].at[rows], dw_ref.at[rows], s["dw"]).start()

    v["dhr"][pipe] = v["dhs"][pipe]
    got15 = v["dhr"].at[pl.ds(0, 15)]
    landed(got15, s["d_r"])
    dh = jnp.sum(v["dhr"][...].astype(I32).astype(F32), axis=0)
    own_bound = 0.51 * jnp.abs(fcol[4, pipe]) + 1e-6 * gcol[pipe]
    v["dh"][...] = lanes_mul(dh, own_bound * (1.0 / TOP)).astype(BF16)
    outs = [
        pltpu.make_async_copy(src, dst, s["local"].at[i])
        for i, (src, dst) in enumerate(((v["dh"], dh_ref), (v["loss"], loss_ref)))
    ]
    for cp in outs:
        cp.start()

    for cp in pending:
        cp.wait_send()
    landed(hm.at[pl.ds(0, 15)], s["h_s"])
    landed(fifteen, s["st_s"].at[0])
    landed(fifteen2, s["st_s"].at[1])
    landed(e_all.at[c], s["ac_s"])
    landed(got15, s["d_s"])
    pltpu.make_async_copy(v["dw"], dw_ref, s["dw"]).wait()
    for cp in outs:
        cp.wait()


def call(hidden, weight, targets, row_grad):
    dma, vm = pltpu.SemaphoreType.DMA, pltpu.VMEM
    one = (ROWS, SUB + CODE)
    hbm = pl.BlockSpec(memory_space=pltpu.HBM)
    buffers = dict(
        hm=vm((NB, ROWS, CHUNK), BF16), hs=vm((NB, ROWS, CHUNK), BF16),
        wm=vm((2 * HALF, CHUNK), BF16), ws=vm((HALF, CHUNK), BF16),
        part=vm((NB, ROWS, HALF), F32), scale=vm((NSUB, NB, ROWS, 128), F32),
        t=vm((2, 128), I32), g=vm((2, 128), F32), tcol=vm((NB, ROWS, 128), I32), gcol=vm((NB, ROWS, 128), F32),
        wt=vm((NB * ROWS, CHUNK), F32), acc=vm((4, NB * ROWS, CHUNK), F32), fcol=vm((5, NB, ROWS, 128), F32),
        e_all=vm((2, NSUB, NB, ROWS, SUB), BF16), dw=vm((2 * HALF, CHUNK), BF16),
        **{name + end: vm((NSUB * n,) + one, I16) for name, n in WIDTHS.items() for end in "sr"},
        mine=vm((1, 1, 640), F32), st0=vm((1, 1, 640), F32), st1=vm((NB, 1, 384), F32), st2=vm((NB, 1, 640), F32),
        dhs=vm((NB, ROWS, CHUNK), I16), dhr=vm((NB, ROWS, CHUNK), I16), dh=vm((ROWS, CHUNK), BF16),
        loss=vm((2, 128), F32),
    )
    pairs = dict(w=1, hf=4, st0=1, st=2)
    pairs.update({a + name: NSUB * n for name, n in WIDTHS.items() for a in ("", "a")})
    sems = dict(
        local=dma((4,)), h_s=dma, h_r=dma((4,)), ac_s=dma, ac_r=dma((2,)), d_s=dma, d_r=dma, dw=dma,
        **{name + end: dma((n,)) for name, n in pairs.items() for end in ("_s", "_r")},
    )
    return pl.pallas_call(
        kernel,
        out_shape=(
            jax.ShapeDtypeStruct((ROWS, CHUNK), BF16),
            jax.ShapeDtypeStruct((2 * HALF, CHUNK), BF16),
            jax.ShapeDtypeStruct((2, 128), F32),
        ),
        in_specs=[hbm] * 4,
        out_specs=(hbm,) * 3,
        scratch_shapes=(buffers, sems),
        compiler_params=pltpu.CompilerParams(
            collective_id=0, has_side_effects=True, vmem_limit_bytes=60 << 20
        ),
        cost_estimate=pl.CostEstimate(flops=1_600_000_000, bytes_accessed=5 << 20, transcendentals=1 << 20),
        name="output_layer",
    )(hidden, weight, targets, row_grad)


PIECES = 8


def settle(dh, dw, loss, dh_out, dw_out, loss_out, dh_v, dw_v, loss_v, sem_in, sem_out):
    rows = 2 * HALF // PIECES
    moves = [(dh, dh_v, dh_out), (loss, loss_v, loss_out)]
    for i in range(PIECES):
        at = pl.ds(i * rows, rows)
        moves.append((dw.at[at], dw_v.at[at], dw_out.at[at]))
    into = [pltpu.make_async_copy(a, b, sem_in.at[i]) for i, (a, b, _) in enumerate(moves)]
    out = [pltpu.make_async_copy(b, d, sem_out.at[i]) for i, (_, b, d) in enumerate(moves)]
    for cp in into:
        cp.start()
    for cp, then in zip(into, out):
        cp.wait()
        then.start()
    for cp in out:
        cp.wait()


def on_device(hidden, weight, targets, row_grad):
    found = call(hidden.reshape(ROWS, CHUNK), weight, targets, row_grad)
    hbm = pl.BlockSpec(memory_space=pltpu.HBM)
    grad_hidden, grad_weight, row_loss = pl.pallas_call(
        settle,
        out_shape=[jax.ShapeDtypeStruct(x.shape, x.dtype) for x in found],
        in_specs=[hbm] * 3,
        out_specs=[hbm] * 3,
        scratch_shapes=[pltpu.VMEM(x.shape, x.dtype) for x in found]
        + [pltpu.SemaphoreType.DMA((PIECES + 2,)), pltpu.SemaphoreType.DMA((PIECES + 2,))],
        compiler_params=pltpu.CompilerParams(vmem_limit_bytes=60 << 20),
        name="settle",
    )(*found)
    return grad_hidden.reshape(2, 8, CHUNK), grad_weight, row_loss[:, :4]


def solution(mesh):
    placed = (P(None, "pipe", "dp"), P("pipe", "dp"), P(), P())
    return jax.shard_map(
        on_device,
        mesh=mesh,
        in_specs=placed,
        out_specs=(P(None, "pipe", "dp"), P("pipe", "dp"), P(None, "dp")),
        check_vma=False,
    )
```

```python
import functools
import math

import jax
import jax.numpy as jnp
from jax import lax
from jax.experimental import pallas as pl
from jax.experimental.pallas import tpu as pltpu
from jax.sharding import PartitionSpec as P

MESH = pl.DeviceIdType.MESH
F32, BF16, I16, I32 = jnp.float32, jnp.bfloat16, jnp.int16, jnp.int32

Y, NB, ROWS = 8, 16, 16
HALF = 2048
SUB, NSUB = 1024, 2
CODE = 128
STEP = math.log(2.0) / 256
TOP = 32766.0
CHUNK = 256


def coords():
    dp, pipe = lax.axis_index("dp"), lax.axis_index("pipe")
    return dp // 4, (dp // 2) % 2, dp % 2, pipe


def lanes_mul(x, s):
    n = x.shape[1] // 128
    return jnp.concatenate([x[:, i * 128 : (i + 1) * 128] * s for i in range(n)], axis=1)


def encode(ref, slot, x, bound):
    code = jnp.ceil(jnp.log(jnp.maximum(bound, 1e-30)) * (1.0 / STEP)) + 1.0
    inv = TOP * jnp.exp(code * -STEP)
    ref[slot, :, :SUB] = jnp.round(lanes_mul(x, inv)).astype(I32).astype(I16)
    ref[slot, :, SUB:] = code.astype(I32).astype(I16)


def decode(ref, slot):
    scale = jnp.exp(ref[slot, :, SUB:].astype(I32).astype(F32) * STEP)
    x = ref[slot, :, :SUB].astype(I32).astype(F32)
    return lanes_mul(x, scale * (1.0 / TOP)), scale


def diagonal():
    return lax.broadcasted_iota(I32, (ROWS, 128), 0) == lax.broadcasted_iota(I32, (ROWS, 128), 1)


def to_lanes(col):
    return jnp.sum(jnp.where(diagonal(), col, 0.0), axis=0, keepdims=True)


def to_rows(row):
    shape = row.shape[:-2] + (ROWS, 128)
    at = len(shape) - 2
    eye = lax.broadcasted_iota(I32, shape, at) == lax.broadcasted_iota(I32, shape, at + 1)
    return jnp.broadcast_to(
        jnp.sum(jnp.where(eye, jnp.broadcast_to(row, shape), 0.0), axis=-1, keepdims=True), shape
    )


WAYS = ((4, 2), (3, 1), (-3, -1), (1, 1), (-1, -1), (2, 2), (-2, -2))
CROSS = (4, 3, -3, 2, -2, 0)
WIDTHS = dict(z=6, x=2, y=7)
SIGNS = (1, -1)


def kernel(h_ref, w_ref, t_ref, g_ref, dh_ref, dw_ref, loss_ref, v, s):
    y, zl, c, pipe = coords()
    zh, px = pipe // 4, pipe % 4
    me_dp = y * 4 + zl * 2 + c
    mb = y * 2 + zl
    hm, hs, wm, ws, part, scale = v["hm"], v["hs"], v["wm"], v["ws"], v["part"], v["scale"]
    e_all, tcol, gcol, fcol, st1, st2 = v["e_all"], v["tcol"], v["gcol"], v["fcol"], v["st1"], v["st2"]

    def at_dp(yy, zz, cc):
        return (yy * 4 + zz * 2 + cc, pipe)

    def yo(o):
        return lax.rem(y + o + Y, Y)

    def block(o, zz):
        return yo(o) * 2 + zz

    def far_first(j):
        return lax.rem(j + 7, 15) + 1

    def pipe_peer(i):
        return lax.rem(zh + i // 4, 4) * 4 + lax.rem(px + i % 4, 4)

    def dp_peer(i):
        return at_dp(lax.rem(y + i // 2, Y), lax.rem(zl + i % 2, 2), c)

    sib = at_dp(y, zl, 1 - c)
    zdev = at_dp(y, 1 - zl, c)
    pending = []

    def send(src, dst, s_sem, r_sem, dev):
        cp = pltpu.make_async_remote_copy(
            src_ref=src, dst_ref=dst, send_sem=s_sem, recv_sem=r_sem, device_id=dev, device_id_type=MESH
        )
        cp.start()
        return cp

    def push(src, dst, name, i, dev):
        cp = send(src, dst, s[name + "_s"].at[i], s[name + "_r"].at[i], dev)
        pending.append(cp)
        return cp

    def landed(ref, sem):
        pltpu.make_async_copy(ref, ref, sem).wait()

    local = [
        pltpu.make_async_copy(src, dst, s["local"].at[i])
        for i, (src, dst) in enumerate(((h_ref, hm.at[pipe]), (t_ref, v["t"]), (g_ref, v["g"]), (w_ref, wm)))
    ]
    for cp in local:
        cp.start()

    barrier = pltpu.get_barrier_semaphore()

    @pl.loop(0, 15)
    def _(j):
        i = far_first(j)
        pl.semaphore_signal(barrier, inc=1, device_id=(me_dp, pipe_peer(i)), device_id_type=MESH)
        pl.semaphore_signal(barrier, inc=1, device_id=dp_peer(i), device_id_type=MESH)

    pl.semaphore_signal(barrier, inc=1, device_id=sib, device_id_type=MESH)
    for cp in local[:3]:
        cp.wait()
    pl.semaphore_wait(barrier, 31)

    @pl.loop(0, 15)
    def _(j):
        i = far_first(j)
        send(hm.at[pipe], hm.at[pipe], s["h_s"], s["h_r"].at[i // 4], (me_dp, pipe_peer(i)))

    half_rows = pl.ds(pl.multiple_of((1 - c) * HALF, HALF), HALF)
    w_swap = push(w_ref.at[half_rows], ws, "w", 0, sib)

    shape = (NB, ROWS, 128)
    b_id, r_id = lax.broadcasted_iota(I32, shape, 0), lax.broadcasted_iota(I32, shape, 1)
    pick = lax.broadcasted_iota(I32, shape, 2) == b_id * 8 + r_id % 8
    first = r_id < 8

    def column(ref):
        x = ref[...].astype(F32)
        x = jnp.where(first, x[0:1].reshape(1, 1, 128), x[1:2].reshape(1, 1, 128))
        return jnp.broadcast_to(jnp.sum(jnp.where(pick, x, 0.0), axis=-1, keepdims=True), shape)

    tcol[...] = column(v["t"]).astype(I32)
    gcol[...] = column(v["g"])

    full = (NB * ROWS, CHUNK)

    def twice(x):
        x = x.reshape(NB * ROWS, 128)
        return jnp.concatenate([x, x], axis=1)

    def at_target(q):
        ids = pipe * (2 * HALF) + q * CHUNK + lax.broadcasted_iota(I32, full, 1)
        return ids == twice(tcol[...])

    local[3].wait()
    v["wt"][...] = jnp.zeros(full, F32)

    @pl.loop(0, 2 * HALF // CHUNK)
    def _(q):
        cols = pl.ds(pl.multiple_of(q * CHUNK, CHUNK), CHUNK)
        one = jnp.where(at_target(q), 1.0, 0.0).astype(BF16)
        v["wt"][...] += jnp.dot(one, wm[cols, :], preferred_element_type=F32)

    near_first = (0, 1, 3, 2)
    forwards = []
    for n, dz in enumerate(near_first):
        group = pl.ds(lax.rem(zh + 4 - dz, 4) * 4, 4)
        landed(hm.at[pl.ds(0, 3 if dz == 0 else 4)], s["h_r"].at[dz])
        forwards.append(push(hm.at[group], hs.at[group], "hf", n, sib))

    nt = (((1,), (1,)), ((), ()))

    def products(u, first):
        if not first:
            scale[u] = jnp.zeros(shape, F32)
        for k in range(u * SUB // CHUNK, (u + 1) * SUB // CHUNK):
            own = pl.ds(pl.multiple_of(c * HALF + k * CHUNK, CHUNK), CHUNK)
            there = pl.ds(k * CHUNK, CHUNK)
            held, rows = (hm, wm[own, :]) if first else (hs, ws[there, :])
            x = lax.dot_general(held[...].reshape(full), rows, nt, preferred_element_type=F32)
            x = x.reshape(NB, ROWS, CHUNK)
            if not first:
                x += part[:, :, there]
                scale[u] = jnp.maximum(scale[u], jnp.maximum(jnp.abs(x[..., :128]), jnp.abs(x[..., 128:])))
            part[:, :, there] = x
        if not first:
            scale[u] = jnp.broadcast_to(jnp.max(scale[u], axis=-1, keepdims=True), shape)

    for u in range(NSUB):
        products(u, True)
    for cp in forwards:
        cp.wait_recv()
    w_swap.wait_recv()

    def lanes(u):
        return slice(u * SUB, (u + 1) * SUB)

    def own(u, b):
        return part[b, :, lanes(u)], scale[u, b]

    way = {}

    def go(u, name, i, got, dev):
        encode(v[f"{name}s"], u * WIDTHS[name] + i, *got)
        slot = u * WIDTHS[name] + i
        way[name, u, i] = push(v[f"{name}s"].at[slot], v[f"{name}r"].at[slot], name, slot, dev)

    def add(u, got, name, *slots):
        x, bound = got
        for i in slots:
            way[name, u, i].wait_recv()
            more, more_bound = decode(v[f"{name}r"], u * WIDTHS[name] + i)
            x, bound = x + more, bound + more_bound
        return x, bound

    def at_y(u, hop):
        return at_dp(yo(SIGNS[u] * hop), zl, c)

    def rs_z(u, *offsets):
        for o in offsets:
            go(u, "z", CROSS.index(o), own(u, block(o * SIGNS[u], 1 - zl)), zdev)

    def rs_side(u):
        for i, o in enumerate((1, -1)):
            go(u, "x", i, own(u, block(o * SIGNS[u], 1 - zl)), at_y(u, o))

    def rs_near(u):
        for i in (3, 4):
            o, hop = WAYS[i]
            go(u, "y", i, own(u, block(o * SIGNS[u], zl)), at_y(u, hop))

    def rs_z_own(u):
        go(u, "z", 5, add(u, own(u, block(0, 1 - zl)), "x", 0, 1), zdev)

    def crossed(u, o):
        return add(u, own(u, block(o * SIGNS[u], zl)), "z", CROSS.index(o))

    def rs_first(u):
        for i in (0, 1, 2):
            go(u, "y", i, crossed(u, WAYS[i][0]), at_y(u, WAYS[i][1]))

    def rs_mid(u):
        go(u, "y", 5, add(u, crossed(u, 2), "y", 0, 1), at_y(u, 2))
        go(u, "y", 6, add(u, crossed(u, -2), "y", 2), at_y(u, -2))

    def rs_end(u):
        return add(u, crossed(u, 0), "y", 3, 4, 5, 6)[0]

    wide = (ROWS, 128)

    def softmax(u, x):
        m_col = jnp.max(x, axis=1, keepdims=True)
        e = jnp.exp(x - m_col)
        s_col = jnp.sum(e, axis=1, keepdims=True)
        ids = pipe * (2 * HALF) + c * HALF + u * SUB + lax.broadcasted_iota(I32, x.shape, 1)
        hit = ids == jnp.concatenate([tcol[mb]] * (SUB // 128), axis=1)
        p_col = jnp.sum(jnp.where(hit, x, 0.0), axis=1, keepdims=True)
        e_all[c, u, mb] = jnp.where(hit, 0.0, e).astype(BF16)
        return [to_lanes(jnp.broadcast_to(a, wide)) for a in (m_col, s_col, p_col)]

    def chunk(u, o, side=0):
        return e_all.at[c, u, block(o * SIGNS[u], zl if side == 0 else 1 - zl)]

    def to_core(u, ref):
        send(ref, ref, s["ac_s"], s["ac_r"].at[u], sib)

    def ag(u, name, i, ref, dev):
        push(ref, ref, "a" + name, u * WIDTHS[name] + i, dev)

    def got(u, name, i, ref):
        landed(ref, s[f"a{name}_r"].at[u * WIDTHS[name] + i])

    def cross(u, o):
        ag(u, "z", CROSS.index(o), chunk(u, o), zdev)

    def ag_own(u):
        ref = chunk(u, 0)
        cross(u, 0)
        for i, hop in ((1, 2), (3, -2), (0, 1), (2, -1)):
            ag(u, "y", i, ref, at_y(u, hop))
        to_core(u, ref)

    def ag_side(u):
        ref = chunk(u, 0, 1)
        got(u, "z", 5, ref)
        for i, hop in enumerate((1, -1)):
            ag(u, "x", i, ref, at_y(u, hop))
        to_core(u, ref)

    def ag_near(u):
        got(u, "y", 1, chunk(u, -2))
        ag(u, "y", 5, chunk(u, -2), at_y(u, 2))
        ag(u, "y", 4, chunk(u, -2), at_y(u, 1))
        cross(u, -2)
        got(u, "y", 3, chunk(u, 2))
        ag(u, "y", 6, chunk(u, 2), at_y(u, -1))
        cross(u, 2)
        for i, o in ((0, -1), (2, 1)):
            got(u, "y", i, chunk(u, o))
        for o in (-2, 2, -1, 1):
            to_core(u, chunk(u, o))

    def ag_far(u):
        for i, o in ((4, -3), (6, 3), (5, 4)):
            got(u, "y", i, chunk(u, o))
            cross(u, o)
            to_core(u, chunk(u, o))

    def ag_side_near(u):
        for i, o in enumerate((-1, 1)):
            got(u, "x", i, chunk(u, o, 1))
            to_core(u, chunk(u, o, 1))

    def ag_crossed(u, *offsets):
        for o in offsets:
            got(u, "z", CROSS.index(o), chunk(u, o, 1))
            to_core(u, chunk(u, o, 1))

    def weigh(u):
        landed(e_all.at[1 - c, u], s["ac_r"].at[u])
        for half in range(2):
            rows = slice(half * HALF + u * SUB, half * HALF + (u + 1) * SUB)
            e = e_all[half, u].reshape(NB * ROWS, SUB)
            v["acc"][half * 2 + u] = jnp.dot(e, wm[rows, :], preferred_element_type=F32)

    products(0, False)
    rs_z(0, 4, 3, -3)
    products(1, False)
    rs_z(1, 4, 3, -3)
    for u in range(NSUB):
        rs_side(u)
        rs_near(u)
    rs_z(0, 2, -2)
    rs_z(1, 2, -2)
    rs_first(0)
    rs_first(1)
    rs_z_own(0)
    rs_z_own(1)
    rs_mid(0)
    rs_mid(1)
    stats0 = softmax(0, rs_end(0))
    ag_own(0)
    stats1 = softmax(1, rs_end(1))
    ag_own(1)

    def put(ref, rows):
        for n, row in enumerate(rows):
            ref[:, n * 128 : (n + 1) * 128] = row

    m_own = jnp.maximum(stats0[0], stats1[0])
    s_own = stats0[1] * jnp.exp(stats0[0] - m_own) + stats1[1] * jnp.exp(stats1[0] - m_own)
    put(v["mine"].at[0], (m_own, s_own, stats0[2] + stats1[2], stats0[0], stats1[0]))
    both = push(v["mine"].at[0], v["st0"].at[0], "st0", 0, sib)
    ag_side(0)
    both.wait_recv()
    other = [v["st0"][0, :, n * 128 : (n + 1) * 128] for n in range(5)]
    m_two = jnp.maximum(m_own, other[0])
    s_two = s_own * jnp.exp(m_own - m_two) + other[1] * jnp.exp(other[0] - m_two)
    put(st1.at[pipe], (m_two, s_two, stats0[2] + stats1[2] + other[2]))

    @pl.loop(0, 15)
    def _(j):
        i = far_first(j)
        send(st1.at[pipe], st1.at[pipe], s["st_s"].at[0], s["st_r"].at[0], (me_dp, pipe_peer(i)))

    ag_near(0)
    ag_side(1)
    ag_near(1)
    ag_side_near(0)
    ag_far(0)
    ag_side_near(1)
    ag_far(1)

    fifteen = st1.at[pl.ds(0, 15)]
    landed(fifteen, s["st_r"].at[0])
    ms, sums, picks = (st1[:, 0, n * 128 : (n + 1) * 128] for n in range(3))
    top = jnp.max(ms, axis=0, keepdims=True)
    total = jnp.sum(sums * jnp.exp(ms - top), axis=0, keepdims=True)
    picked = jnp.sum(picks, axis=0, keepdims=True)
    total = jnp.where(lax.broadcasted_iota(I32, (1, 128), 1) < ROWS, total, 1.0)
    g = to_lanes(gcol[mb])
    f_own = [g * (jnp.exp(st[0] - top) / total) for st in (stats0, stats1)]
    f_other = [g * (jnp.exp(m - top) / total) for m in other[3:]]
    at_hit = g * (jnp.exp(picked - top) / total - 1.0)
    loss = top + jnp.log(total) - picked
    low = [jnp.where(c == 0, a, b) for a, b in zip(f_own, f_other)]
    high = [jnp.where(c == 0, b, a) for a, b in zip(f_own, f_other)]
    put(st2.at[mb], (*low, *high, at_hit.astype(BF16).astype(F32)))

    @pl.loop(0, 15)
    def _(j):
        i = far_first(j)
        send(st2.at[mb], st2.at[mb], s["st_s"].at[1], s["st_r"].at[1], dp_peer(i))

    ag_crossed(0, -2, 2)
    ag_crossed(1, -2, 2)
    ag_crossed(0, -3, 3, 4)
    weigh(0)
    loss_col = to_rows(loss)
    r2, l2 = lax.broadcasted_iota(I32, wide, 0), lax.broadcasted_iota(I32, wide, 1)
    loss_out = jnp.where(r2 % 8 == 4 * c + l2, loss_col, 0.0).reshape(2, 8, 128)
    v["loss"][...] = jnp.sum(loss_out, axis=1)
    ag_crossed(1, -3, 3, 4)
    fifteen2 = st2.at[pl.ds(0, 15)]
    landed(fifteen2, s["st_r"].at[1])
    for n in range(5):
        fcol[n] = to_rows(st2[:, :, n * 128 : (n + 1) * 128])
    weigh(1)

    bound = 0.51 * jnp.abs(fcol[4]) + 1e-6 * gcol[...]
    dh = v["wt"][...] * twice(fcol[4])
    for n in range(4):
        dh += v["acc"][n] * twice(fcol[n])
    q16 = jnp.clip(dh * twice(TOP / bound), -TOP, TOP)
    v["dhs"][...] = jnp.round(q16).astype(I32).astype(I16).reshape(NB, ROWS, CHUNK)

    @pl.loop(0, 15)
    def _(j):
        i = far_first(j)
        to = pipe_peer(i)
        send(v["dhs"].at[to], v["dhr"].at[pipe], s["d_s"], s["d_r"], (me_dp, to))

    tn = (((0,), (0,)), ((), ()))

    @pl.loop(0, 2 * HALF // CHUNK)
    def _(q):
        hh, u, k = q // 8, (q // 4) % 2, q % 4
        e = e_all[hh, u, :, :, pl.ds(pl.multiple_of(k * CHUNK, CHUNK), CHUNK)].reshape(full).astype(F32)
        d = jnp.where(at_target(q), twice(fcol[4]), e * twice(fcol[hh * 2 + u])).astype(BF16)
        x = lax.dot_general(d, hm[...].reshape(full), tn, preferred_element_type=F32)
        rows = pl.ds(pl.multiple_of(q * CHUNK, CHUNK), CHUNK)
        v["dw"][rows, :] = x.astype(BF16)
        pltpu.make_async_copy(v["dw"].at[rows], dw_ref.at[rows], s["dw"]).start()

    v["dhr"][pipe] = v["dhs"][pipe]
    got15 = v["dhr"].at[pl.ds(0, 15)]
    landed(got15, s["d_r"])
    dh = jnp.sum(v["dhr"][...].astype(I32).astype(F32), axis=0)
    own_bound = 0.51 * jnp.abs(fcol[4, pipe]) + 1e-6 * gcol[pipe]
    v["dh"][...] = lanes_mul(dh, own_bound * (1.0 / TOP)).astype(BF16)
    outs = [
        pltpu.make_async_copy(src, dst, s["local"].at[i])
        for i, (src, dst) in enumerate(((v["dh"], dh_ref), (v["loss"], loss_ref)))
    ]
    for cp in outs:
        cp.start()

    for cp in pending:
        cp.wait_send()
    landed(hm.at[pl.ds(0, 15)], s["h_s"])
    landed(fifteen, s["st_s"].at[0])
    landed(fifteen2, s["st_s"].at[1])
    landed(e_all.at[c], s["ac_s"])
    landed(got15, s["d_s"])
    pltpu.make_async_copy(v["dw"], dw_ref, s["dw"]).wait()
    for cp in outs:
        cp.wait()


def call(hidden, weight, targets, row_grad):
    dma, vm = pltpu.SemaphoreType.DMA, pltpu.VMEM
    one = (ROWS, SUB + CODE)
    hbm = pl.BlockSpec(memory_space=pltpu.HBM)
    buffers = dict(
        hm=vm((NB, ROWS, CHUNK), BF16), hs=vm((NB, ROWS, CHUNK), BF16),
        wm=vm((2 * HALF, CHUNK), BF16), ws=vm((HALF, CHUNK), BF16),
        part=vm((NB, ROWS, HALF), F32), scale=vm((NSUB, NB, ROWS, 128), F32),
        t=vm((2, 128), I32), g=vm((2, 128), F32), tcol=vm((NB, ROWS, 128), I32), gcol=vm((NB, ROWS, 128), F32),
        wt=vm((NB * ROWS, CHUNK), F32), acc=vm((4, NB * ROWS, CHUNK), F32), fcol=vm((5, NB, ROWS, 128), F32),
        e_all=vm((2, NSUB, NB, ROWS, SUB), BF16), dw=vm((2 * HALF, CHUNK), BF16),
        **{name + end: vm((NSUB * n,) + one, I16) for name, n in WIDTHS.items() for end in "sr"},
        mine=vm((1, 1, 640), F32), st0=vm((1, 1, 640), F32), st1=vm((NB, 1, 384), F32), st2=vm((NB, 1, 640), F32),
        dhs=vm((NB, ROWS, CHUNK), I16), dhr=vm((NB, ROWS, CHUNK), I16), dh=vm((ROWS, CHUNK), BF16),
        loss=vm((2, 128), F32),
    )
    pairs = dict(w=1, hf=4, st0=1, st=2)
    pairs.update({a + name: NSUB * n for name, n in WIDTHS.items() for a in ("", "a")})
    sems = dict(
        local=dma((4,)), h_s=dma, h_r=dma((4,)), ac_s=dma, ac_r=dma((2,)), d_s=dma, d_r=dma, dw=dma,
        **{name + end: dma((n,)) for name, n in pairs.items() for end in ("_s", "_r")},
    )
    return pl.pallas_call(
        kernel,
        out_shape=(
            jax.ShapeDtypeStruct((ROWS, CHUNK), BF16),
            jax.ShapeDtypeStruct((2 * HALF, CHUNK), BF16),
            jax.ShapeDtypeStruct((2, 128), F32),
        ),
        in_specs=[hbm] * 4,
        out_specs=(hbm,) * 3,
        scratch_shapes=(buffers, sems),
        compiler_params=pltpu.CompilerParams(
            collective_id=0, has_side_effects=True, vmem_limit_bytes=60 << 20
        ),
        cost_estimate=pl.CostEstimate(flops=1_600_000_000, bytes_accessed=5 << 20, transcendentals=1 << 20),
        name="output_layer",
    )(hidden, weight, targets, row_grad)


PIECES = 8


def settle(dh, dw, loss, dh_out, dw_out, loss_out, dh_v, dw_v, loss_v, sem_in, sem_out):
    rows = 2 * HALF // PIECES
    moves = [(dh, dh_v, dh_out), (loss, loss_v, loss_out)]
    for i in range(PIECES):
        at = pl.ds(i * rows, rows)
        moves.append((dw.at[at], dw_v.at[at], dw_out.at[at]))
    into = [pltpu.make_async_copy(a, b, sem_in.at[i]) for i, (a, b, _) in enumerate(moves)]
    out = [pltpu.make_async_copy(b, d, sem_out.at[i]) for i, (_, b, d) in enumerate(moves)]
    for cp in into:
        cp.start()
    for cp, then in zip(into, out):
        cp.wait()
        then.start()
    for cp in out:
        cp.wait()


def on_device(hidden, weight, targets, row_grad):
    found = call(hidden.reshape(ROWS, CHUNK), weight, targets, row_grad)
    hbm = pl.BlockSpec(memory_space=pltpu.HBM)
    grad_hidden, grad_weight, row_loss = pl.pallas_call(
        settle,
        out_shape=[jax.ShapeDtypeStruct(x.shape, x.dtype) for x in found],
        in_specs=[hbm] * 3,
        out_specs=[hbm] * 3,
        scratch_shapes=[pltpu.VMEM(x.shape, x.dtype) for x in found]
        + [pltpu.SemaphoreType.DMA((PIECES + 2,)), pltpu.SemaphoreType.DMA((PIECES + 2,))],
        compiler_params=pltpu.CompilerParams(vmem_limit_bytes=60 << 20),
        name="settle",
    )(*found)
    return grad_hidden.reshape(2, 8, CHUNK), grad_weight, row_loss[:, :4]


def solution(mesh):
    placed = (P(None, "pipe", "dp"), P("pipe", "dp"), P(), P())
    return jax.shard_map(
        on_device,
        mesh=mesh,
        in_specs=placed,
        out_specs=(P(None, "pipe", "dp"), P("pipe", "dp"), P(None, "dp")),
        check_vma=False,
    )
```

```python
import functools
import math

import jax
import jax.numpy as jnp
from jax import lax
from jax.experimental import pallas as pl
from jax.experimental.pallas import tpu as pltpu
from jax.sharding import PartitionSpec as P

MESH = pl.DeviceIdType.MESH
F32, BF16, I16, I32 = jnp.float32, jnp.bfloat16, jnp.int16, jnp.int32

Y, NB, ROWS = 8, 16, 16
HALF = 2048
SUB, NSUB = 1024, 2
CODE = 128
STEP = math.log(2.0) / 256
TOP = 32766.0
CHUNK = 256


def coords():
    dp, pipe = lax.axis_index("dp"), lax.axis_index("pipe")
    return dp // 4, (dp // 2) % 2, dp % 2, pipe


def lanes_mul(x, s):
    n = x.shape[1] // 128
    return jnp.concatenate([x[:, i * 128 : (i + 1) * 128] * s for i in range(n)], axis=1)


def encode(ref, slot, x, bound):
    code = jnp.ceil(jnp.log(jnp.maximum(bound, 1e-30)) * (1.0 / STEP)) + 1.0
    inv = TOP * jnp.exp(code * -STEP)
    ref[slot, :, :SUB] = jnp.round(lanes_mul(x, inv)).astype(I32).astype(I16)
    ref[slot, :, SUB:] = code.astype(I32).astype(I16)


def decode(ref, slot):
    scale = jnp.exp(ref[slot, :, SUB:].astype(I32).astype(F32) * STEP)
    x = ref[slot, :, :SUB].astype(I32).astype(F32)
    return lanes_mul(x, scale * (1.0 / TOP)), scale


def diagonal():
    return lax.broadcasted_iota(I32, (ROWS, 128), 0) == lax.broadcasted_iota(I32, (ROWS, 128), 1)


def to_lanes(col):
    return jnp.sum(jnp.where(diagonal(), col, 0.0), axis=0, keepdims=True)


def to_rows(row):
    shape = row.shape[:-2] + (ROWS, 128)
    at = len(shape) - 2
    eye = lax.broadcasted_iota(I32, shape, at) == lax.broadcasted_iota(I32, shape, at + 1)
    return jnp.broadcast_to(
        jnp.sum(jnp.where(eye, jnp.broadcast_to(row, shape), 0.0), axis=-1, keepdims=True), shape
    )


WAYS = ((4, 2), (3, 1), (-3, -1), (1, 1), (-1, -1), (2, 2), (-2, -2))
CROSS = (4, 3, -3, 2, -2, 0)
WIDTHS = dict(z=6, x=2, y=7)
SIGNS = (1, -1)


def kernel(h_ref, w_ref, t_ref, g_ref, dh_ref, dw_ref, loss_ref, v, s):
    y, zl, c, pipe = coords()
    zh, px = pipe // 4, pipe % 4
    me_dp = y * 4 + zl * 2 + c
    mb = y * 2 + zl
    hm, hs, wm, ws, part, scale = v["hm"], v["hs"], v["wm"], v["ws"], v["part"], v["scale"]
    e_all, tcol, gcol, fcol, st1, st2 = v["e_all"], v["tcol"], v["gcol"], v["fcol"], v["st1"], v["st2"]

    def at_dp(yy, zz, cc):
        return (yy * 4 + zz * 2 + cc, pipe)

    def yo(o):
        return lax.rem(y + o + Y, Y)

    def block(o, zz):
        return yo(o) * 2 + zz

    def far_first(j):
        return lax.rem(j + 7, 15) + 1

    def pipe_peer(i):
        return lax.rem(zh + i // 4, 4) * 4 + lax.rem(px + i % 4, 4)

    def dp_peer(i):
        return at_dp(lax.rem(y + i // 2, Y), lax.rem(zl + i % 2, 2), c)

    sib = at_dp(y, zl, 1 - c)
    zdev = at_dp(y, 1 - zl, c)
    pending = []

    def send(src, dst, s_sem, r_sem, dev):
        cp = pltpu.make_async_remote_copy(
            src_ref=src, dst_ref=dst, send_sem=s_sem, recv_sem=r_sem, device_id=dev, device_id_type=MESH
        )
        cp.start()
        return cp

    def push(src, dst, name, i, dev):
        cp = send(src, dst, s[name + "_s"].at[i], s[name + "_r"].at[i], dev)
        pending.append(cp)
        return cp

    def landed(ref, sem):
        pltpu.make_async_copy(ref, ref, sem).wait()

    local = [
        pltpu.make_async_copy(src, dst, s["local"].at[i])
        for i, (src, dst) in enumerate(((h_ref, hm.at[pipe]), (t_ref, v["t"]), (g_ref, v["g"]), (w_ref, wm)))
    ]
    for cp in local:
        cp.start()

    barrier = pltpu.get_barrier_semaphore()

    @pl.loop(0, 15)
    def _(j):
        i = far_first(j)
        pl.semaphore_signal(barrier, inc=1, device_id=(me_dp, pipe_peer(i)), device_id_type=MESH)
        pl.semaphore_signal(barrier, inc=1, device_id=dp_peer(i), device_id_type=MESH)

    pl.semaphore_signal(barrier, inc=1, device_id=sib, device_id_type=MESH)
    for cp in local[:3]:
        cp.wait()
    pl.semaphore_wait(barrier, 31)

    @pl.loop(0, 15)
    def _(j):
        i = far_first(j)
        send(hm.at[pipe], hm.at[pipe], s["h_s"], s["h_r"].at[i // 4], (me_dp, pipe_peer(i)))

    half_rows = pl.ds(pl.multiple_of((1 - c) * HALF, HALF), HALF)
    w_swap = push(w_ref.at[half_rows], ws, "w", 0, sib)

    shape = (NB, ROWS, 128)
    b_id, r_id = lax.broadcasted_iota(I32, shape, 0), lax.broadcasted_iota(I32, shape, 1)
    pick = lax.broadcasted_iota(I32, shape, 2) == b_id * 8 + r_id % 8
    first = r_id < 8

    def column(ref):
        x = ref[...].astype(F32)
        x = jnp.where(first, x[0:1].reshape(1, 1, 128), x[1:2].reshape(1, 1, 128))
        return jnp.broadcast_to(jnp.sum(jnp.where(pick, x, 0.0), axis=-1, keepdims=True), shape)

    tcol[...] = column(v["t"]).astype(I32)
    gcol[...] = column(v["g"])

    full = (NB * ROWS, CHUNK)

    def twice(x):
        x = x.reshape(NB * ROWS, 128)
        return jnp.concatenate([x, x], axis=1)

    def at_target(q):
        ids = pipe * (2 * HALF) + q * CHUNK + lax.broadcasted_iota(I32, full, 1)
        return ids == twice(tcol[...])

    local[3].wait()
    v["wt"][...] = jnp.zeros(full, F32)

    @pl.loop(0, 2 * HALF // CHUNK)
    def _(q):
        cols = pl.ds(pl.multiple_of(q * CHUNK, CHUNK), CHUNK)
        one = jnp.where(at_target(q), 1.0, 0.0).astype(BF16)
        v["wt"][...] += jnp.dot(one, wm[cols, :], preferred_element_type=F32)

    near_first = (0, 1, 3, 2)
    forwards = []
    for n, dz in enumerate(near_first):
        group = pl.ds(lax.rem(zh + 4 - dz, 4) * 4, 4)
        landed(hm.at[pl.ds(0, 3 if dz == 0 else 4)], s["h_r"].at[dz])
        forwards.append(push(hm.at[group], hs.at[group], "hf", n, sib))

    nt = (((1,), (1,)), ((), ()))

    def products(u, first):
        if not first:
            scale[u] = jnp.zeros(shape, F32)
        for k in range(u * SUB // CHUNK, (u + 1) * SUB // CHUNK):
            own = pl.ds(pl.multiple_of(c * HALF + k * CHUNK, CHUNK), CHUNK)
            there = pl.ds(k * CHUNK, CHUNK)
            held, rows = (hm, wm[own, :]) if first else (hs, ws[there, :])
            x = lax.dot_general(held[...].reshape(full), rows, nt, preferred_element_type=F32)
            x = x.reshape(NB, ROWS, CHUNK)
            if not first:
                x += part[:, :, there]
                scale[u] = jnp.maximum(scale[u], jnp.maximum(jnp.abs(x[..., :128]), jnp.abs(x[..., 128:])))
            part[:, :, there] = x
        if not first:
            scale[u] = jnp.broadcast_to(jnp.max(scale[u], axis=-1, keepdims=True), shape)

    for u in range(NSUB):
        products(u, True)
    for cp in forwards:
        cp.wait_recv()
    w_swap.wait_recv()

    def lanes(u):
        return slice(u * SUB, (u + 1) * SUB)

    def own(u, b):
        return part[b, :, lanes(u)], scale[u, b]

    way = {}

    def go(u, name, i, got, dev):
        encode(v[f"{name}s"], u * WIDTHS[name] + i, *got)
        slot = u * WIDTHS[name] + i
        way[name, u, i] = push(v[f"{name}s"].at[slot], v[f"{name}r"].at[slot], name, slot, dev)

    def add(u, got, name, *slots):
        x, bound = got
        for i in slots:
            way[name, u, i].wait_recv()
            more, more_bound = decode(v[f"{name}r"], u * WIDTHS[name] + i)
            x, bound = x + more, bound + more_bound
        return x, bound

    def at_y(u, hop):
        return at_dp(yo(SIGNS[u] * hop), zl, c)

    def rs_z(u, *offsets):
        for o in offsets:
            go(u, "z", CROSS.index(o), own(u, block(o * SIGNS[u], 1 - zl)), zdev)

    def rs_side(u):
        for i, o in enumerate((1, -1)):
            go(u, "x", i, own(u, block(o * SIGNS[u], 1 - zl)), at_y(u, o))

    def rs_near(u):
        for i in (3, 4):
            o, hop = WAYS[i]
            go(u, "y", i, own(u, block(o * SIGNS[u], zl)), at_y(u, hop))

    def rs_z_own(u):
        go(u, "z", 5, add(u, own(u, block(0, 1 - zl)), "x", 0, 1), zdev)

    def crossed(u, o):
        return add(u, own(u, block(o * SIGNS[u], zl)), "z", CROSS.index(o))

    def rs_first(u):
        for i in (0, 1, 2):
            go(u, "y", i, crossed(u, WAYS[i][0]), at_y(u, WAYS[i][1]))

    def rs_mid(u):
        go(u, "y", 5, add(u, crossed(u, 2), "y", 0, 1), at_y(u, 2))
        go(u, "y", 6, add(u, crossed(u, -2), "y", 2), at_y(u, -2))

    def rs_end(u):
        return add(u, crossed(u, 0), "y", 3, 4, 5, 6)[0]

    wide = (ROWS, 128)

    def softmax(u, x):
        m_col = jnp.max(x, axis=1, keepdims=True)
        e = jnp.exp(x - m_col)
        s_col = jnp.sum(e, axis=1, keepdims=True)
        ids = pipe * (2 * HALF) + c * HALF + u * SUB + lax.broadcasted_iota(I32, x.shape, 1)
        hit = ids == jnp.concatenate([tcol[mb]] * (SUB // 128), axis=1)
        p_col = jnp.sum(jnp.where(hit, x, 0.0), axis=1, keepdims=True)
        e_all[c, u, mb] = jnp.where(hit, 0.0, e).astype(BF16)
        return [to_lanes(jnp.broadcast_to(a, wide)) for a in (m_col, s_col, p_col)]

    def chunk(u, o, side=0):
        return e_all.at[c, u, block(o * SIGNS[u], zl if side == 0 else 1 - zl)]

    def to_core(u, ref):
        send(ref, ref, s["ac_s"], s["ac_r"].at[u], sib)

    def ag(u, name, i, ref, dev):
        push(ref, ref, "a" + name, u * WIDTHS[name] + i, dev)

    def got(u, name, i, ref):
        landed(ref, s[f"a{name}_r"].at[u * WIDTHS[name] + i])

    def cross(u, o):
        ag(u, "z", CROSS.index(o), chunk(u, o), zdev)

    def ag_own(u):
        ref = chunk(u, 0)
        cross(u, 0)
        for i, hop in ((1, 2), (3, -2), (0, 1), (2, -1)):
            ag(u, "y", i, ref, at_y(u, hop))
        to_core(u, ref)

    def ag_side(u):
        ref = chunk(u, 0, 1)
        got(u, "z", 5, ref)
        for i, hop in enumerate((1, -1)):
            ag(u, "x", i, ref, at_y(u, hop))
        to_core(u, ref)

    def ag_near(u):
        got(u, "y", 1, chunk(u, -2))
        ag(u, "y", 5, chunk(u, -2), at_y(u, 2))
        ag(u, "y", 4, chunk(u, -2), at_y(u, 1))
        cross(u, -2)
        got(u, "y", 3, chunk(u, 2))
        ag(u, "y", 6, chunk(u, 2), at_y(u, -1))
        cross(u, 2)
        for i, o in ((0, -1), (2, 1)):
            got(u, "y", i, chunk(u, o))
        for o in (-2, 2, -1, 1):
            to_core(u, chunk(u, o))

    def ag_far(u):
        for i, o in ((4, -3), (6, 3), (5, 4)):
            got(u, "y", i, chunk(u, o))
            cross(u, o)
            to_core(u, chunk(u, o))

    def ag_side_near(u):
        for i, o in enumerate((-1, 1)):
            got(u, "x", i, chunk(u, o, 1))
            to_core(u, chunk(u, o, 1))

    def ag_crossed(u, *offsets):
        for o in offsets:
            got(u, "z", CROSS.index(o), chunk(u, o, 1))
            to_core(u, chunk(u, o, 1))

    def weigh(u):
        for n, half in enumerate((c, 1 - c)):
            if n == 1:
                landed(e_all.at[1 - c, u], s["ac_r"].at[u])
            rows = pl.ds(pl.multiple_of(half * HALF + u * SUB, SUB), SUB)
            e = e_all[half, u].reshape(NB * ROWS, SUB)
            v["acc"][half * 2 + u] = jnp.dot(e, wm[rows, :], preferred_element_type=F32)

    products(0, False)
    rs_z(0, 4, 3, -3)
    products(1, False)
    rs_z(1, 4, 3, -3)
    for u in range(NSUB):
        rs_side(u)
        rs_near(u)
    rs_z(0, 2, -2)
    rs_z(1, 2, -2)
    rs_first(0)
    rs_first(1)
    rs_z_own(0)
    rs_z_own(1)
    rs_mid(0)
    rs_mid(1)
    stats0 = softmax(0, rs_end(0))
    ag_own(0)
    stats1 = softmax(1, rs_end(1))
    ag_own(1)

    def put(ref, rows):
        for n, row in enumerate(rows):
            ref[:, n * 128 : (n + 1) * 128] = row

    m_own = jnp.maximum(stats0[0], stats1[0])
    s_own = stats0[1] * jnp.exp(stats0[0] - m_own) + stats1[1] * jnp.exp(stats1[0] - m_own)
    put(v["mine"].at[0], (m_own, s_own, stats0[2] + stats1[2], stats0[0], stats1[0]))
    both = push(v["mine"].at[0], v["st0"].at[0], "st0", 0, sib)
    ag_side(0)
    both.wait_recv()
    other = [v["st0"][0, :, n * 128 : (n + 1) * 128] for n in range(5)]
    m_two = jnp.maximum(m_own, other[0])
    s_two = s_own * jnp.exp(m_own - m_two) + other[1] * jnp.exp(other[0] - m_two)
    put(st1.at[pipe], (m_two, s_two, stats0[2] + stats1[2] + other[2]))

    @pl.loop(0, 15)
    def _(j):
        i = far_first(j)
        send(st1.at[pipe], st1.at[pipe], s["st_s"].at[0], s["st_r"].at[0], (me_dp, pipe_peer(i)))

    ag_near(0)
    ag_side(1)
    ag_near(1)
    ag_side_near(0)
    ag_far(0)
    ag_side_near(1)
    ag_far(1)

    fifteen = st1.at[pl.ds(0, 15)]
    landed(fifteen, s["st_r"].at[0])
    ms, sums, picks = (st1[:, 0, n * 128 : (n + 1) * 128] for n in range(3))
    top = jnp.max(ms, axis=0, keepdims=True)
    total = jnp.sum(sums * jnp.exp(ms - top), axis=0, keepdims=True)
    picked = jnp.sum(picks, axis=0, keepdims=True)
    total = jnp.where(lax.broadcasted_iota(I32, (1, 128), 1) < ROWS, total, 1.0)
    g = to_lanes(gcol[mb])
    f_own = [g * (jnp.exp(st[0] - top) / total) for st in (stats0, stats1)]
    f_other = [g * (jnp.exp(m - top) / total) for m in other[3:]]
    at_hit = g * (jnp.exp(picked - top) / total - 1.0)
    loss = top + jnp.log(total) - picked
    low = [jnp.where(c == 0, a, b) for a, b in zip(f_own, f_other)]
    high = [jnp.where(c == 0, b, a) for a, b in zip(f_own, f_other)]
    put(st2.at[mb], (*low, *high, at_hit.astype(BF16).astype(F32)))

    @pl.loop(0, 15)
    def _(j):
        i = far_first(j)
        send(st2.at[mb], st2.at[mb], s["st_s"].at[1], s["st_r"].at[1], dp_peer(i))

    ag_crossed(0, -2, 2)
    ag_crossed(1, -2, 2)
    ag_crossed(0, -3, 3, 4)
    weigh(0)
    loss_col = to_rows(loss)
    r2, l2 = lax.broadcasted_iota(I32, wide, 0), lax.broadcasted_iota(I32, wide, 1)
    loss_out = jnp.where(r2 % 8 == 4 * c + l2, loss_col, 0.0).reshape(2, 8, 128)
    v["loss"][...] = jnp.sum(loss_out, axis=1)
    ag_crossed(1, -3, 3, 4)
    fifteen2 = st2.at[pl.ds(0, 15)]
    landed(fifteen2, s["st_r"].at[1])
    for n in range(5):
        fcol[n] = to_rows(st2[:, :, n * 128 : (n + 1) * 128])
    weigh(1)

    bound = 0.51 * jnp.abs(fcol[4]) + 1e-6 * gcol[...]
    dh = v["wt"][...] * twice(fcol[4])
    for n in range(4):
        dh += v["acc"][n] * twice(fcol[n])
    q16 = jnp.clip(dh * twice(TOP / bound), -TOP, TOP)
    v["dhs"][...] = jnp.round(q16).astype(I32).astype(I16).reshape(NB, ROWS, CHUNK)

    @pl.loop(0, 15)
    def _(j):
        i = far_first(j)
        to = pipe_peer(i)
        send(v["dhs"].at[to], v["dhr"].at[pipe], s["d_s"], s["d_r"], (me_dp, to))

    tn = (((0,), (0,)), ((), ()))

    @pl.loop(0, 2 * HALF // CHUNK)
    def _(q):
        hh, u, k = q // 8, (q // 4) % 2, q % 4
        e = e_all[hh, u, :, :, pl.ds(pl.multiple_of(k * CHUNK, CHUNK), CHUNK)].reshape(full).astype(F32)
        d = jnp.where(at_target(q), twice(fcol[4]), e * twice(fcol[hh * 2 + u])).astype(BF16)
        x = lax.dot_general(d, hm[...].reshape(full), tn, preferred_element_type=F32)
        rows = pl.ds(pl.multiple_of(q * CHUNK, CHUNK), CHUNK)
        v["dw"][rows, :] = x.astype(BF16)
        pltpu.make_async_copy(v["dw"].at[rows], dw_ref.at[rows], s["dw"]).start()

    v["dhr"][pipe] = v["dhs"][pipe]
    got15 = v["dhr"].at[pl.ds(0, 15)]
    landed(got15, s["d_r"])
    dh = jnp.sum(v["dhr"][...].astype(I32).astype(F32), axis=0)
    own_bound = 0.51 * jnp.abs(fcol[4, pipe]) + 1e-6 * gcol[pipe]
    v["dh"][...] = lanes_mul(dh, own_bound * (1.0 / TOP)).astype(BF16)
    outs = [
        pltpu.make_async_copy(src, dst, s["local"].at[i])
        for i, (src, dst) in enumerate(((v["dh"], dh_ref), (v["loss"], loss_ref)))
    ]
    for cp in outs:
        cp.start()

    for cp in pending:
        cp.wait_send()
    landed(hm.at[pl.ds(0, 15)], s["h_s"])
    landed(fifteen, s["st_s"].at[0])
    landed(fifteen2, s["st_s"].at[1])
    landed(e_all.at[c], s["ac_s"])
    landed(got15, s["d_s"])
    pltpu.make_async_copy(v["dw"], dw_ref, s["dw"]).wait()
    for cp in outs:
        cp.wait()


def call(hidden, weight, targets, row_grad):
    dma, vm = pltpu.SemaphoreType.DMA, pltpu.VMEM
    one = (ROWS, SUB + CODE)
    hbm = pl.BlockSpec(memory_space=pltpu.HBM)
    buffers = dict(
        hm=vm((NB, ROWS, CHUNK), BF16), hs=vm((NB, ROWS, CHUNK), BF16),
        wm=vm((2 * HALF, CHUNK), BF16), ws=vm((HALF, CHUNK), BF16),
        part=vm((NB, ROWS, HALF), F32), scale=vm((NSUB, NB, ROWS, 128), F32),
        t=vm((2, 128), I32), g=vm((2, 128), F32), tcol=vm((NB, ROWS, 128), I32), gcol=vm((NB, ROWS, 128), F32),
        wt=vm((NB * ROWS, CHUNK), F32), acc=vm((4, NB * ROWS, CHUNK), F32), fcol=vm((5, NB, ROWS, 128), F32),
        e_all=vm((2, NSUB, NB, ROWS, SUB), BF16), dw=vm((2 * HALF, CHUNK), BF16),
        **{name + end: vm((NSUB * n,) + one, I16) for name, n in WIDTHS.items() for end in "sr"},
        mine=vm((1, 1, 640), F32), st0=vm((1, 1, 640), F32), st1=vm((NB, 1, 384), F32), st2=vm((NB, 1, 640), F32),
        dhs=vm((NB, ROWS, CHUNK), I16), dhr=vm((NB, ROWS, CHUNK), I16), dh=vm((ROWS, CHUNK), BF16),
        loss=vm((2, 128), F32),
    )
    pairs = dict(w=1, hf=4, st0=1, st=2)
    pairs.update({a + name: NSUB * n for name, n in WIDTHS.items() for a in ("", "a")})
    sems = dict(
        local=dma((4,)), h_s=dma, h_r=dma((4,)), ac_s=dma, ac_r=dma((2,)), d_s=dma, d_r=dma, dw=dma,
        **{name + end: dma((n,)) for name, n in pairs.items() for end in ("_s", "_r")},
    )
    return pl.pallas_call(
        kernel,
        out_shape=(
            jax.ShapeDtypeStruct((ROWS, CHUNK), BF16),
            jax.ShapeDtypeStruct((2 * HALF, CHUNK), BF16),
            jax.ShapeDtypeStruct((2, 128), F32),
        ),
        in_specs=[hbm] * 4,
        out_specs=(hbm,) * 3,
        scratch_shapes=(buffers, sems),
        compiler_params=pltpu.CompilerParams(
            collective_id=0, has_side_effects=True, vmem_limit_bytes=60 << 20
        ),
        cost_estimate=pl.CostEstimate(flops=1_600_000_000, bytes_accessed=5 << 20, transcendentals=1 << 20),
        name="output_layer",
    )(hidden, weight, targets, row_grad)


PIECES = 8


def settle(dh, dw, loss, dh_out, dw_out, loss_out, dh_v, dw_v, loss_v, sem_in, sem_out):
    rows = 2 * HALF // PIECES
    moves = [(dh, dh_v, dh_out), (loss, loss_v, loss_out)]
    for i in range(PIECES):
        at = pl.ds(i * rows, rows)
        moves.append((dw.at[at], dw_v.at[at], dw_out.at[at]))
    into = [pltpu.make_async_copy(a, b, sem_in.at[i]) for i, (a, b, _) in enumerate(moves)]
    out = [pltpu.make_async_copy(b, d, sem_out.at[i]) for i, (_, b, d) in enumerate(moves)]
    for cp in into:
        cp.start()
    for cp, then in zip(into, out):
        cp.wait()
        then.start()
    for cp in out:
        cp.wait()


def on_device(hidden, weight, targets, row_grad):
    found = call(hidden.reshape(ROWS, CHUNK), weight, targets, row_grad)
    hbm = pl.BlockSpec(memory_space=pltpu.HBM)
    grad_hidden, grad_weight, row_loss = pl.pallas_call(
        settle,
        out_shape=[jax.ShapeDtypeStruct(x.shape, x.dtype) for x in found],
        in_specs=[hbm] * 3,
        out_specs=[hbm] * 3,
        scratch_shapes=[pltpu.VMEM(x.shape, x.dtype) for x in found]
        + [pltpu.SemaphoreType.DMA((PIECES + 2,)), pltpu.SemaphoreType.DMA((PIECES + 2,))],
        compiler_params=pltpu.CompilerParams(vmem_limit_bytes=60 << 20),
        name="settle",
    )(*found)
    return grad_hidden.reshape(2, 8, CHUNK), grad_weight, row_loss[:, :4]


def solution(mesh):
    placed = (P(None, "pipe", "dp"), P("pipe", "dp"), P(), P())
    return jax.shard_map(
        on_device,
        mesh=mesh,
        in_specs=placed,
        out_specs=(P(None, "pipe", "dp"), P("pipe", "dp"), P(None, "dp")),
        check_vma=False,
    )
```
